32 devices in a mesh: pts: 16 (over z, y, x), blk: 2 (over core).
Axes of the slice: x: 2, y: 2, z: 4, core: 2. Of those that a mesh axis runs over, the one named last changes fastest.
Arguments:
- deviations: bfloat16 [196608, 256], P(('pts', 'blk')), may hold values from -6 to 6
- basis: bfloat16 [196608, 64], P(('pts', 'blk')), may hold values from -0.013671875 to 0.013671875
- sensitivity: bfloat16 [64, 512, 512], P('pts', 'blk'), may hold values from -0.75 to 0.75
- blade_ids: int32 [24], replicated, may hold values from 0 to 255, as said below
Outputs:
- gram: float32 [256, 256], P('pts', 'blk')
- change: float32 [24, 512, 512], P(None, 'blk', 'pts')
The draws below stay inside these ranges and needn't reach their ends.
Inputs may be any that keep to these rules, and one draw needn't show every extreme that they name: `blade_ids`: distinct blade numbers; blade 0 and blade 256 - 1 are always among them.
All inputs are finite; a program needn't handle non-finite values.
Results may differ from the reference program's by a relative error of at most 0.0003.
Values may be sent and summed in bfloat16 or wider, within the bound.
A program may use at most 64 MiB of HBM per device.

```python
import jax
import jax.numpy as jnp
from jax import lax

NBLADE = 256
NSHAPE = 64
ORDER = 512
NREAL = 24
ROWS = 6144
NPTS = 196608


def draw_blade_ids(key, part):
    first_key, second_key = jax.random.split(key)
    inner = jax.random.permutation(first_key, NBLADE - 2)[:NREAL - 2] + 1
    chosen = jnp.concatenate([inner.astype(jnp.int32), jnp.array([0, NBLADE - 1], jnp.int32)])
    return jax.random.permutation(second_key, chosen).astype(jnp.int32)


def spiked(values, own_key, source, target, blocks, factor):
    def block_of(axis_at):
        return (jnp.arange(values.shape[axis_at]) // (values.shape[axis_at] // blocks)).reshape((-1,) + (1,) * (values.ndim - 1 - axis_at))

    near = jax.random.permutation(own_key, blocks)[block_of(target)]
    far = (block_of(target) + blocks // 2) % blocks
    return jnp.where((block_of(source) == near) | (block_of(source) == far), factor * values, values)


def level_of(own_key, shape, shards, least, largest):
    def one(dim, parts):
        heights = jax.random.uniform(jax.random.fold_in(jax.random.fold_in(own_key, 6), dim), (parts,), jnp.float32, least / len(shards), largest / len(shards))
        return jnp.repeat(jnp.exp(heights), shape[dim] // parts).reshape((-1,) + (1,) * (len(shape) - dim - 1))

    gain = one(*shards[0])
    for cut in shards[1:]:
        gain = gain * one(*cut)
    return gain


def noise(key, shape, scale, bound, cuts=(), held_as=jnp.bfloat16):
    result = jax.random.normal(key, shape, jnp.float32) * scale
    if len(cuts) > 0:
        result = level_of(key, shape, cuts, -0.22, 0.18) * result
    return jnp.clip(result, min=-bound, max=bound).astype(held_as)


def bell_draw_with(stream_key, shape, width, most, shards, heavy, held_as=jnp.bfloat16):
    values = width * jax.random.normal(stream_key, shape, jnp.float32)
    if shards:
        values = values * level_of(stream_key, shape, shards, -0.22, 0.18)
    return jnp.clip(spiked(values, jax.random.fold_in(stream_key, 3), *heavy), -most, most).astype(held_as)


def setup_inputs(seed: int = 0) -> dict:
    key_list = jax.random.split(jax.random.key(seed), 5)
    deviations = bell_draw_with(key_list[0], (NPTS, NBLADE), 1.0, 6.0, ((0, 32),), (0, 1, 32, 2.75))
    basis = noise(key_list[1], (NPTS, NSHAPE), NPTS ** -0.5, 0.013671875, ((0, 32),))
    sensitivity = noise(key_list[2], (NSHAPE, ORDER, ORDER), NSHAPE ** -0.5, 0.75, ((0, 16), (1, 2)))
    blade_ids = draw_blade_ids(jax.random.fold_in(key_list[4], 71), 0)
    return {"deviations": deviations, "basis": basis, "sensitivity": sensitivity, "blade_ids": blade_ids}


def reference(deviations, basis, sensitivity, blade_ids):
    count = NPTS // ROWS

    def accumulate(index, carry):
        gram_sum, coeff_sum, energy_sum = carry
        start = (index * ROWS).astype(jnp.int32)
        block = lax.dynamic_slice_in_dim(deviations, start, ROWS, 0)
        shapes = lax.dynamic_slice_in_dim(basis, start, ROWS, 0)
        dims = (((0,), (0,)), ((), ()))
        gram_sum = gram_sum + lax.dot_general(block, block, dims, preferred_element_type=jnp.float32)
        coeff_sum = coeff_sum + lax.dot_general(shapes, block, dims, preferred_element_type=jnp.float32)
        wide = block.astype(jnp.float32)
        energy_sum = energy_sum + lax.optimization_barrier(jnp.sum(wide * wide, axis=0))
        return (gram_sum, coeff_sum, energy_sum)
    init = (jnp.zeros((NBLADE, NBLADE), jnp.float32), jnp.zeros((NSHAPE, NBLADE), jnp.float32), jnp.zeros((NBLADE,), jnp.float32))
    gram_sum, coeffs, energy_sum = lax.fori_loop(0, count, accumulate, init)
    gram = gram_sum / NPTS
    energy = energy_sum / NPTS
    weights = coeffs[:, blade_ids] / jnp.sqrt(energy[blade_ids] + 1e-05)
    change = jnp.einsum('kb,kij->bij', weights, sensitivity.astype(jnp.float32), precision=lax.Precision.HIGHEST)
    return (gram, change)
```

```python
import functools

import jax
import jax.numpy as jnp
from jax import lax
from jax.experimental import pallas as pl
from jax.experimental.pallas import tpu as pltpu
from jax.sharding import PartitionSpec as P

MESH = pl.DeviceIdType.MESH
F32 = jnp.float32
BF16 = jnp.bfloat16
GROUP = 16
EPS = 1e-05


def split_of(count):
    inner = 1
    while inner * inner < count:
        inner *= 2
    return count // inner, inner


def kernel(
    dims, ids_ref, dev_hbm, basis_hbm, sens_hbm, gram_ref, change_ref,
    dev_v, basis_v, sens_v, turned, blocks, gram_acc, coef_acc, w_hi, w_lo,
    s1, r1, s2, r2, s3, r3,
    dev_sem, basis_sem, sens_sem, own_sem, a_send, a_recv, c_send, c_recv, x_send, x_recv, z_send, z_recv,
):
    outer, inner, chunks, total = dims
    count = outer * inner
    half = outer // 2
    me = lax.axis_index("pts")
    core = lax.axis_index("blk")
    o, i = me // inner, me % inner
    side = o // half
    reals = ids_ref.shape[1]
    points, blades = dev_hbm.shape
    shapes = basis_hbm.shape[0]
    own, rows, order = sens_hbm.shape
    cols = order // count
    part = points // chunks
    gram_rows, gram_cols = gram_ref.shape
    span = order // 2

    far = pl.multiple_of((1 - side) * span, 128)
    near = pl.multiple_of(side * span, 128)
    loads = []
    for at, start in enumerate((far, near)):
        loads.append(
            pltpu.make_async_copy(
                sens_hbm.at[:, :, pl.ds(start, span)], sens_v.at[:, :, pl.ds(start, span)], sens_sem.at[at]
            )
        )
        loads[-1].start()
    basis_load = pltpu.make_async_copy(basis_hbm, basis_v, basis_sem)
    basis_load.start()

    def dev_load(c):
        at = pl.ds(pl.multiple_of(c * part, part), part)
        return pltpu.make_async_copy(dev_hbm.at[at], dev_v.at[at], dev_sem.at[c])

    for c in range(chunks):
        dev_load(c).start()

    barrier = pltpu.get_barrier_semaphore()
    for d in range(1, count):
        pl.semaphore_signal(barrier, inc=1, device_id=((me + d) % count, core), device_id_type=MESH)
    pl.semaphore_signal(barrier, inc=1, device_id=(me, 1 - core), device_id_type=MESH)

    def turn(start):
        for k in range(own):
            turned[k, pl.ds(start, span), :] = sens_v[k, :, pl.ds(start, span)].T

    def block_to(peer):
        at = pl.ds(pl.multiple_of(peer * cols, cols), cols)
        return pltpu.make_async_remote_copy(
            src_ref=turned.at[:, at, :], dst_ref=blocks.at[me], send_sem=a_send.at[peer], recv_sem=a_recv.at[me],
            device_id=(peer, core), device_id_type=MESH,
        )

    def block_from(peer):
        return pltpu.make_async_remote_copy(
            src_ref=turned.at[:, pl.ds(0, cols), :], dst_ref=blocks.at[peer], send_sem=a_send.at[peer],
            recv_sem=a_recv.at[peer], device_id=(peer, core), device_id_type=MESH,
        )

    far_planes = [(1 - side) * half + (o + e) % half for e in range(half)]
    near_planes = [side * half + (o + e) % half for e in range(half)]

    loads[0].wait()
    turn(far)
    pl.semaphore_wait(barrier, count)
    sent = []
    for plane in far_planes:
        for e in range(inner):
            sent.append(block_to(plane * inner + (i + e) % inner))
            sent[-1].start()
    loads[1].wait()
    turn(near)
    for at, plane in reversed(list(enumerate(near_planes))):
        for e in range(inner):
            if at == 0 and e == 0:
                continue
            sent.append(block_to(plane * inner + (i + e) % inner))
            sent[-1].start()
    mine = pltpu.make_async_copy(
        turned.at[:, pl.ds(pl.multiple_of(me * cols, cols), cols), :], blocks.at[me], own_sem
    )
    mine.start()

    gram_acc[...] = jnp.zeros_like(gram_acc)
    coef_acc[...] = jnp.zeros_like(coef_acc)
    basis_load.wait()

    def accumulate(c, carry):
        dev_load(c).wait()
        start = pl.multiple_of(c * part, part)
        block = dev_v[pl.ds(start, part), :]
        gram_acc[...] += jnp.dot(block.T, block, preferred_element_type=F32)
        coef_acc[0:shapes, :] += jnp.dot(basis_v[:, pl.ds(start, part)], block, preferred_element_type=F32)
        return carry

    lax.fori_loop(0, chunks, accumulate, 0)

    wide = coef_acc.shape[0]
    ids = jnp.broadcast_to(ids_ref[...].astype(F32), (reals, reals))
    square = lax.broadcasted_iota(jnp.int32, (reals, reals), 0) == lax.broadcasted_iota(jnp.int32, (reals, reals), 1)
    ids_col = jnp.sum(jnp.where(square, ids, 0.0), axis=1, keepdims=True)
    lane = lax.broadcasted_iota(jnp.int32, (reals, blades), 1).astype(F32)
    chosen = jnp.where(ids_col == lane, 1.0, 0.0).astype(F32)
    gram = gram_acc[...]
    diagonal = lax.broadcasted_iota(jnp.int32, gram.shape, 0) == lax.broadcasted_iota(jnp.int32, gram.shape, 1)
    squares = jnp.sum(jnp.where(diagonal, gram, 0.0), axis=0, keepdims=True)
    energy = jnp.sum(chosen * squares, axis=1, keepdims=True)
    picked = lax.dot_general(
        chosen, coef_acc[...], (((1,), (1,)), ((), ())), preferred_element_type=F32, precision=lax.Precision.HIGHEST
    )
    place = lax.broadcasted_iota(jnp.int32, (reals, wide), 1)
    picked = jnp.where(place < shapes, picked, energy)

    for h in range(2):
        s1[h, 0:blades, :] = gram[:, h * gram_cols:(h + 1) * gram_cols]
        s1[h, blades:blades + reals, :] = picked
    over = pltpu.make_async_remote_copy(
        src_ref=s1.at[1 - core], dst_ref=r1, send_sem=c_send, recv_sem=c_recv,
        device_id=(me, 1 - core), device_id_type=MESH,
    )
    over.start()
    over.wait_recv()

    body = outer * gram_rows
    tail = s1[core, blades:blades + reals, :] + r1[blades:blades + reals, :]
    for j in range(inner):
        for q in range(outer):
            at = (q * inner + j) * gram_rows
            s2[j, q * gram_rows:(q + 1) * gram_rows, :] = (
                s1[core, at:at + gram_rows, :] + r1[at:at + gram_rows, :]
            )
        s2[j, body:body + reals, :] = tail
    plane_sent = []
    for e in range(1, inner):
        j = (i + e) % inner
        plane_sent.append(
            pltpu.make_async_remote_copy(
                src_ref=s2.at[j], dst_ref=r2.at[i], send_sem=x_send.at[j], recv_sem=x_recv.at[i],
                device_id=(o * inner + j, core), device_id_type=MESH,
            )
        )
        plane_sent[-1].start()
    value = s2[i]
    for e in range(1, inner):
        j = (i + e) % inner
        pltpu.make_async_remote_copy(
            src_ref=s2.at[j], dst_ref=r2.at[j], send_sem=x_send.at[j], recv_sem=x_recv.at[j],
            device_id=(o * inner + j, core), device_id_type=MESH,
        ).wait_recv()
        value = value + r2[j]

    for q in range(outer):
        s3[q, 0:gram_rows, :] = value[q * gram_rows:(q + 1) * gram_rows, :]
        s3[q, gram_rows:gram_rows + reals, :] = value[body:body + reals, :]
    out_sent = []
    for e in range(1, outer):
        q = (o + e) % outer
        out_sent.append(
            pltpu.make_async_remote_copy(
                src_ref=s3.at[q], dst_ref=r3.at[o], send_sem=z_send.at[q], recv_sem=z_recv.at[o],
                device_id=(q * inner + i, core), device_id_type=MESH,
            )
        )
        out_sent[-1].start()
    value = s3[o]
    for e in range(1, outer):
        q = (o + e) % outer
        pltpu.make_async_remote_copy(
            src_ref=s3.at[q], dst_ref=r3.at[q], send_sem=z_send.at[q], recv_sem=z_recv.at[q],
            device_id=(q * inner + i, core), device_id_type=MESH,
        ).wait_recv()
        value = value + r3[q]
    gram_ref[...] = value[0:gram_rows, :] / total

    packed = value[gram_rows:gram_rows + reals, :]
    moved = pltpu.roll(packed, wide - shapes, 1)
    weights = jnp.where(place < shapes, packed / jnp.sqrt(jnp.where(place < shapes, moved, 0.0) / total + EPS), 0.0)
    tall = jnp.broadcast_to(weights[:, None, :], (reals, GROUP, wide)).reshape(reals * GROUP, wide)
    hi = tall.astype(BF16)
    lo = (tall - hi.astype(F32)).astype(BF16)
    long = shapes * GROUP
    spread = (
        lax.broadcasted_iota(jnp.int32, (wide, long), 1) // GROUP == lax.broadcasted_iota(jnp.int32, (wide, long), 0)
    ).astype(F32).astype(BF16)
    keep = (
        lax.broadcasted_iota(jnp.int32, (reals * GROUP, long), 0) % GROUP
        == lax.broadcasted_iota(jnp.int32, (reals * GROUP, long), 1) % GROUP
    )
    w_hi[...] = jnp.where(keep, jnp.dot(hi, spread, preferred_element_type=F32), 0.0).astype(BF16)
    w_lo[...] = jnp.where(keep, jnp.dot(lo, spread, preferred_element_type=F32), 0.0).astype(BF16)

    mine.wait()
    step = inner * own * GROUP
    for at, plane in enumerate(near_planes + far_planes):
        for e in range(inner):
            if at == 0 and e == 0:
                continue
            block_from(plane * inner + (i + e) % inner).wait_recv()
        lanes = pl.ds(pl.multiple_of(plane * step, step), step)
        left_hi, left_lo = w_hi[:, lanes], w_lo[:, lanes]
        for g in range(cols // GROUP):
            here = slice(g * GROUP, (g + 1) * GROUP)
            right = blocks[pl.ds(plane * inner, inner), :, here, :].reshape(step, rows)
            term = jnp.dot(left_hi, right, preferred_element_type=F32) + jnp.dot(
                left_lo, right, preferred_element_type=F32
            )
            term = term.reshape(reals, GROUP, rows)
            if at == 0:
                change_ref[:, here, :] = term
            else:
                change_ref[:, here, :] += term

    over.wait_send()
    for copy in sent + plane_sent + out_sent:
        copy.wait_send()


def in_kernel(deviations, basis, sensitivity, blade_ids):
    count = lax.axis_size("pts")
    cores = lax.axis_size("blk")
    points, blades = deviations.shape
    shapes = basis.shape[1]
    own, rows, order = sensitivity.shape
    reals = blade_ids.shape[0]
    outer, inner = split_of(count)
    cols = order // count
    gram_rows, gram_cols = blades // count, blades // cores
    chunks = 12
    wide = 2 * shapes
    total = float(points * count * cores)
    hbm = pl.BlockSpec(memory_space=pltpu.HBM)
    vmem = pl.BlockSpec(memory_space=pltpu.VMEM)
    sem = pltpu.SemaphoreType.DMA
    body = outer * gram_rows
    flops = 2 * points * blades * (blades + shapes) + 4 * reals * shapes * GROUP * rows * cols
    gram, change = pl.pallas_call(
        functools.partial(kernel, (outer, inner, chunks, total)),
        out_shape=(
            jax.ShapeDtypeStruct((gram_rows, gram_cols), F32),
            jax.ShapeDtypeStruct((reals, cols, rows), F32),
        ),
        in_specs=[vmem, hbm, hbm, hbm],
        out_specs=(vmem, vmem),
        scratch_shapes=[
            pltpu.VMEM((points, blades), BF16),
            pltpu.VMEM((shapes, points), BF16),
            pltpu.VMEM((own, rows, order), BF16),
            pltpu.VMEM((own, order, rows), BF16),
            pltpu.VMEM((count, own, cols, rows), BF16),
            pltpu.VMEM((blades, blades), F32),
            pltpu.VMEM((wide, blades), F32),
            pltpu.VMEM((reals * GROUP, shapes * GROUP), BF16),
            pltpu.VMEM((reals * GROUP, shapes * GROUP), BF16),
            pltpu.VMEM((2, blades + reals, gram_cols), F32),
            pltpu.VMEM((blades + reals, gram_cols), F32),
            pltpu.VMEM((inner, body + reals, gram_cols), F32),
            pltpu.VMEM((inner, body + reals, gram_cols), F32),
            pltpu.VMEM((outer, gram_rows + reals, gram_cols), F32),
            pltpu.VMEM((outer, gram_rows + reals, gram_cols), F32),
            sem((chunks,)), sem, sem((2,)), sem,
            sem((count,)), sem((count,)), sem, sem,
            sem((inner,)), sem((inner,)), sem((outer,)), sem((outer,)),
        ],
        compiler_params=pltpu.CompilerParams(
            collective_id=0, has_side_effects=True, vmem_limit_bytes=60 * 1024 * 1024
        ),
        cost_estimate=pl.CostEstimate(
            flops=flops, transcendentals=0, bytes_accessed=2 * points * (blades + shapes) + 8 * own * rows * order
        ),
    )(blade_ids[None, :], deviations, basis.T, sensitivity)
    return gram, jnp.transpose(change, (0, 2, 1))


def with_collectives(deviations, basis, sensitivity, blade_ids):
    total = deviations.shape[0] * lax.axis_size("pts") * lax.axis_size("blk")
    blades = deviations.shape[1]
    dims = (((0,), (0,)), ((), ()))
    term = lax.dot_general(deviations, deviations, dims, preferred_element_type=F32) / total
    row_part = lax.psum_scatter(term, "pts", scatter_dimension=0, tiled=True)
    gram = lax.psum_scatter(row_part, "blk", scatter_dimension=1, tiled=True)
    coeff_part = lax.dot_general(basis, deviations, dims, preferred_element_type=F32)
    energy_part = jnp.sum(jnp.square(deviations.astype(F32)), axis=0) / total
    selector = (jnp.arange(blades, dtype=jnp.int32)[:, None] == blade_ids[None, :]).astype(F32)
    coeffs, energy = lax.psum((coeff_part, energy_part), ("pts", "blk"))
    picked = jnp.dot(coeffs, selector, precision=lax.Precision.HIGHEST)
    picked_energy = jnp.dot(energy, selector, precision=lax.Precision.HIGHEST)
    weights = picked / jnp.sqrt(picked_energy + EPS)
    tiles = lax.all_to_all(sensitivity, "pts", split_axis=2, concat_axis=0, tiled=True)
    change = jnp.einsum("kb,kij->bij", weights, tiles.astype(F32), precision=lax.Precision.HIGHEST)
    return gram, change


def on_device(deviations, basis, sensitivity, blade_ids):
    count, cores = lax.axis_size("pts"), lax.axis_size("blk")
    points, blades = deviations.shape
    own, rows, order = sensitivity.shape
    outer, inner = split_of(count)
    fits = (
        cores == 2
        and outer * inner == count
        and outer % 2 == 0
        and (order // count) % GROUP == 0
        and (blades // count) % 8 == 0
        and (blades // cores) == 2 * basis.shape[1]
        and (blades // cores) % 128 == 0
        and rows % 128 == 0
        and order % 256 == 0
        and (inner * own * GROUP) % 128 == 0
        and points % (12 * 128) == 0
        and blade_ids.shape[0] % 8 == 0
    )
    run = in_kernel if fits else with_collectives
    return run(deviations, basis, sensitivity, blade_ids)


def solution(mesh):
    in_specs = (P(("pts", "blk"), None), P(("pts", "blk"), None), P("pts", "blk", None), P())
    out_specs = (P("pts", "blk"), P(None, "blk", "pts"))
    return jax.shard_map(
        on_device, mesh=mesh, in_specs=in_specs, out_specs=out_specs, check_vma=False
    )
```

```python
import functools

import jax
import jax.numpy as jnp
from jax import lax
from jax.experimental import pallas as pl
from jax.experimental.pallas import tpu as pltpu
from jax.sharding import PartitionSpec as P

MESH = pl.DeviceIdType.MESH
F32 = jnp.float32
BF16 = jnp.bfloat16
GROUP = 16
EPS = 1e-05


def split_of(count):
    inner = 1
    while inner * inner < count:
        inner *= 2
    return count // inner, inner


def kernel(
    dims, ids_hbm, dev_hbm, basis_hbm, sens_hbm, gram_ref, change_ref,
    ids_ref, dev_v, basis_v, sens_v, turned, blocks, gram_acc, coef_acc, spread_v, keep_v, w_hi, w_lo,
    s1, r1, s2, r2, s3, r3,
    ids_sem, dev_sem, basis_sem, sens_sem, own_sem, a_send, a_recv, c_send, c_recv, x_send, x_recv, z_send, z_recv,
):
    outer, inner, chunks, total = dims
    count = outer * inner
    half = outer // 2
    me = lax.axis_index("pts")
    core = lax.axis_index("blk")
    o, i = me // inner, me % inner
    side = o // half
    reals = ids_ref.shape[1]
    points, blades = dev_hbm.shape
    shapes = basis_hbm.shape[0]
    own, rows, order = sens_hbm.shape
    cols = order // count
    part = points // chunks
    gram_rows, gram_cols = gram_ref.shape
    span = order // 2

    barrier = pltpu.get_barrier_semaphore()
    for d in range(1, count):
        pl.semaphore_signal(barrier, inc=1, device_id=((me + d) % count, core), device_id_type=MESH)
    pl.semaphore_signal(barrier, inc=1, device_id=(me, 1 - core), device_id_type=MESH)

    far = pl.multiple_of((1 - side) * span, 128)
    near = pl.multiple_of(side * span, 128)
    loads = []
    for at, start in enumerate((far, near)):
        loads.append(
            pltpu.make_async_copy(
                sens_hbm.at[:, :, pl.ds(start, span)], sens_v.at[:, :, pl.ds(start, span)], sens_sem.at[at]
            )
        )
        loads[-1].start()
    ids_load = pltpu.make_async_copy(ids_hbm, ids_ref, ids_sem)
    ids_load.start()
    basis_load = pltpu.make_async_copy(basis_hbm, basis_v, basis_sem)
    basis_load.start()

    def dev_load(c):
        at = pl.ds(pl.multiple_of(c * part, part), part)
        return pltpu.make_async_copy(dev_hbm.at[at], dev_v.at[at], dev_sem.at[c])

    for c in range(chunks):
        dev_load(c).start()

    def turn(start):
        for k in range(own):
            turned[k, pl.ds(start, span), :] = sens_v[k, :, pl.ds(start, span)].T

    def block_to(peer):
        at = pl.ds(pl.multiple_of(peer * cols, cols), cols)
        return pltpu.make_async_remote_copy(
            src_ref=turned.at[:, at, :], dst_ref=blocks.at[me], send_sem=a_send.at[peer], recv_sem=a_recv.at[me],
            device_id=(peer, core), device_id_type=MESH,
        )

    def block_from(peer):
        return pltpu.make_async_remote_copy(
            src_ref=turned.at[:, pl.ds(0, cols), :], dst_ref=blocks.at[peer], send_sem=a_send.at[peer],
            recv_sem=a_recv.at[peer], device_id=(peer, core), device_id_type=MESH,
        )

    far_planes = [(1 - side) * half + (o + e) % half for e in range(half)]
    near_planes = [side * half + (o + e) % half for e in range(half)]

    loads[0].wait()
    turn(far)
    pl.semaphore_wait(barrier, count)
    sent = []
    for plane in far_planes:
        for e in range(inner):
            sent.append(block_to(plane * inner + (i + e) % inner))
            sent[-1].start()
    loads[1].wait()
    turn(near)
    for at, plane in reversed(list(enumerate(near_planes))):
        for e in range(inner):
            if at == 0 and e == 0:
                continue
            sent.append(block_to(plane * inner + (i + e) % inner))
            sent[-1].start()
    mine = pltpu.make_async_copy(
        turned.at[:, pl.ds(pl.multiple_of(me * cols, cols), cols), :], blocks.at[me], own_sem
    )
    mine.start()

    spread_v[...] = (
        lax.broadcasted_iota(jnp.int32, spread_v.shape, 1) // GROUP == lax.broadcasted_iota(jnp.int32, spread_v.shape, 0)
    ).astype(F32).astype(BF16)
    keep_v[...] = (
        lax.broadcasted_iota(jnp.int32, keep_v.shape, 0) % GROUP
        == lax.broadcasted_iota(jnp.int32, keep_v.shape, 1) % GROUP
    ).astype(F32).astype(BF16)

    gram_acc[...] = jnp.zeros_like(gram_acc)
    coef_acc[...] = jnp.zeros_like(coef_acc)
    basis_load.wait()

    def accumulate(c, carry):
        dev_load(c).wait()
        start = pl.multiple_of(c * part, part)
        block = dev_v[pl.ds(start, part), :]
        gram_acc[...] += jnp.dot(block.T, block, preferred_element_type=F32)
        coef_acc[0:shapes, :] += jnp.dot(basis_v[:, pl.ds(start, part)], block, preferred_element_type=F32)
        return carry

    lax.fori_loop(0, chunks, accumulate, 0)

    wide = coef_acc.shape[0]
    ids_load.wait()
    ids = jnp.broadcast_to(ids_ref[...].astype(F32), (reals, reals))
    square = lax.broadcasted_iota(jnp.int32, (reals, reals), 0) == lax.broadcasted_iota(jnp.int32, (reals, reals), 1)
    ids_col = jnp.sum(jnp.where(square, ids, 0.0), axis=1, keepdims=True)
    lane = lax.broadcasted_iota(jnp.int32, (reals, blades), 1).astype(F32)
    chosen = jnp.where(ids_col == lane, 1.0, 0.0).astype(F32)
    gram = gram_acc[...]
    diagonal = lax.broadcasted_iota(jnp.int32, gram.shape, 0) == lax.broadcasted_iota(jnp.int32, gram.shape, 1)
    squares = jnp.sum(jnp.where(diagonal, gram, 0.0), axis=0, keepdims=True)
    energy = jnp.sum(chosen * squares, axis=1, keepdims=True)
    picked = lax.dot_general(
        chosen, coef_acc[...], (((1,), (1,)), ((), ())), preferred_element_type=F32, precision=lax.Precision.HIGHEST
    )
    place = lax.broadcasted_iota(jnp.int32, (reals, wide), 1)
    picked = jnp.where(place < shapes, picked, energy)

    for h in range(2):
        s1[h, 0:blades, :] = gram[:, h * gram_cols:(h + 1) * gram_cols]
        s1[h, blades:blades + reals, :] = picked
    over = pltpu.make_async_remote_copy(
        src_ref=s1.at[1 - core], dst_ref=r1, send_sem=c_send, recv_sem=c_recv,
        device_id=(me, 1 - core), device_id_type=MESH,
    )
    over.start()
    over.wait_recv()

    body = outer * gram_rows
    tail = s1[core, blades:blades + reals, :] + r1[blades:blades + reals, :]
    for j in range(inner):
        for q in range(outer):
            at = (q * inner + j) * gram_rows
            s2[j, q * gram_rows:(q + 1) * gram_rows, :] = (
                s1[core, at:at + gram_rows, :] + r1[at:at + gram_rows, :]
            )
        s2[j, body:body + reals, :] = tail
    plane_sent = []
    for e in range(1, inner):
        j = (i + e) % inner
        plane_sent.append(
            pltpu.make_async_remote_copy(
                src_ref=s2.at[j], dst_ref=r2.at[i], send_sem=x_send.at[j], recv_sem=x_recv.at[i],
                device_id=(o * inner + j, core), device_id_type=MESH,
            )
        )
        plane_sent[-1].start()
    value = s2[i]
    for e in range(1, inner):
        j = (i + e) % inner
        pltpu.make_async_remote_copy(
            src_ref=s2.at[j], dst_ref=r2.at[j], send_sem=x_send.at[j], recv_sem=x_recv.at[j],
            device_id=(o * inner + j, core), device_id_type=MESH,
        ).wait_recv()
        value = value + r2[j]

    for q in range(outer):
        s3[q, 0:gram_rows, :] = value[q * gram_rows:(q + 1) * gram_rows, :]
        s3[q, gram_rows:gram_rows + reals, :] = value[body:body + reals, :]
    out_sent = []
    for e in range(1, outer):
        q = (o + e) % outer
        out_sent.append(
            pltpu.make_async_remote_copy(
                src_ref=s3.at[q], dst_ref=r3.at[o], send_sem=z_send.at[q], recv_sem=z_recv.at[o],
                device_id=(q * inner + i, core), device_id_type=MESH,
            )
        )
        out_sent[-1].start()
    value = s3[o]
    for e in range(1, outer):
        q = (o + e) % outer
        pltpu.make_async_remote_copy(
            src_ref=s3.at[q], dst_ref=r3.at[q], send_sem=z_send.at[q], recv_sem=z_recv.at[q],
            device_id=(q * inner + i, core), device_id_type=MESH,
        ).wait_recv()
        value = value + r3[q]
    gram_ref[...] = value[0:gram_rows, :] / total

    packed = value[gram_rows:gram_rows + reals, :]
    moved = pltpu.roll(packed, wide - shapes, 1)
    weights = jnp.where(place < shapes, packed / jnp.sqrt(jnp.where(place < shapes, moved, 0.0) / total + EPS), 0.0)
    tall = jnp.broadcast_to(weights[:, None, :], (reals, GROUP, wide)).reshape(reals * GROUP, wide)
    hi = tall.astype(BF16)
    lo = (tall - hi.astype(F32)).astype(BF16)
    spread = spread_v[...]
    w_hi[...] = jnp.dot(hi, spread, preferred_element_type=F32).astype(BF16) * keep_v[...]
    w_lo[...] = jnp.dot(lo, spread, preferred_element_type=F32).astype(BF16) * keep_v[...]

    mine.wait()
    step = inner * own * GROUP
    for at, plane in enumerate(near_planes + far_planes):
        for e in range(inner):
            if at == 0 and e == 0:
                continue
            block_from(plane * inner + (i + e) % inner).wait_recv()
        lanes = pl.ds(pl.multiple_of(plane * step, step), step)
        left_hi, left_lo = w_hi[:, lanes], w_lo[:, lanes]
        for g in range(cols // GROUP):
            here = slice(g * GROUP, (g + 1) * GROUP)
            right = blocks[pl.ds(plane * inner, inner), :, here, :].reshape(step, rows)
            term = jnp.dot(left_hi, right, preferred_element_type=F32) + jnp.dot(
                left_lo, right, preferred_element_type=F32
            )
            term = term.reshape(reals, GROUP, rows)
            if at == 0:
                change_ref[:, here, :] = term
            else:
                change_ref[:, here, :] += term

    over.wait_send()
    for copy in sent + plane_sent + out_sent:
        copy.wait_send()


def hand_over(pieces, gram_ref, change_ref, gram_out, change_out, sems):
    part = change_ref.shape[0] // pieces
    copies = [pltpu.make_async_copy(gram_ref, gram_out, sems.at[pieces])]
    for at in range(pieces):
        here = pl.ds(at * part, part)
        copies.append(pltpu.make_async_copy(change_ref.at[here], change_out.at[here], sems.at[at]))
    for copy in copies:
        copy.start()
    for copy in copies:
        copy.wait()


def in_kernel(deviations, basis, sensitivity, blade_ids):
    count = lax.axis_size("pts")
    cores = lax.axis_size("blk")
    points, blades = deviations.shape
    shapes = basis.shape[1]
    own, rows, order = sensitivity.shape
    reals = blade_ids.shape[0]
    outer, inner = split_of(count)
    cols = order // count
    gram_rows, gram_cols = blades // count, blades // cores
    chunks = 12
    wide = 2 * shapes
    total = float(points * count * cores)
    hbm = pl.BlockSpec(memory_space=pltpu.HBM)
    vmem = pl.BlockSpec(memory_space=pltpu.VMEM)
    sem = pltpu.SemaphoreType.DMA
    body = outer * gram_rows
    flops = 2 * points * blades * (blades + shapes) + 4 * reals * shapes * GROUP * rows * cols
    gram, change = pl.pallas_call(
        functools.partial(kernel, (outer, inner, chunks, total)),
        out_shape=(pltpu.VMEM((gram_rows, gram_cols), F32), pltpu.VMEM((reals, cols, rows), F32)),
        in_specs=[hbm, hbm, hbm, hbm],
        out_specs=(vmem, vmem),
        scratch_shapes=[
            pltpu.VMEM((1, reals), jnp.int32),
            pltpu.VMEM((points, blades), BF16),
            pltpu.VMEM((shapes, points), BF16),
            pltpu.VMEM((own, rows, order), BF16),
            pltpu.VMEM((own, order, rows), BF16),
            pltpu.VMEM((count, own, cols, rows), BF16),
            pltpu.VMEM((blades, blades), F32),
            pltpu.VMEM((wide, blades), F32),
            pltpu.VMEM((wide, shapes * GROUP), BF16),
            pltpu.VMEM((reals * GROUP, shapes * GROUP), BF16),
            pltpu.VMEM((reals * GROUP, shapes * GROUP), BF16),
            pltpu.VMEM((reals * GROUP, shapes * GROUP), BF16),
            pltpu.VMEM((2, blades + reals, gram_cols), F32),
            pltpu.VMEM((blades + reals, gram_cols), F32),
            pltpu.VMEM((inner, body + reals, gram_cols), F32),
            pltpu.VMEM((inner, body + reals, gram_cols), F32),
            pltpu.VMEM((outer, gram_rows + reals, gram_cols), F32),
            pltpu.VMEM((outer, gram_rows + reals, gram_cols), F32),
            sem, sem((chunks,)), sem, sem((2,)), sem,
            sem((count,)), sem((count,)), sem, sem,
            sem((inner,)), sem((inner,)), sem((outer,)), sem((outer,)),
        ],
        compiler_params=pltpu.CompilerParams(
            collective_id=0, has_side_effects=True, vmem_limit_bytes=32 * 1024 * 1024
        ),
        cost_estimate=pl.CostEstimate(
            flops=flops, transcendentals=0, bytes_accessed=2 * points * (blades + shapes) + 8 * own * rows * order
        ),
    )(
        pltpu.with_memory_space_constraint(blade_ids[None, :], pltpu.HBM),
        pltpu.with_memory_space_constraint(deviations, pltpu.HBM),
        pltpu.with_memory_space_constraint(basis.T, pltpu.HBM),
        pltpu.with_memory_space_constraint(sensitivity, pltpu.HBM),
    )
    pieces = 4
    gram, change = pl.pallas_call(
        functools.partial(hand_over, pieces),
        out_shape=(
            jax.ShapeDtypeStruct((gram_rows, gram_cols), F32),
            jax.ShapeDtypeStruct((reals, cols, rows), F32),
        ),
        in_specs=[vmem, vmem],
        out_specs=(hbm, hbm),
        scratch_shapes=[sem((pieces + 1,))],
    )(gram, change)
    return gram, jnp.transpose(change, (0, 2, 1))


def with_collectives(deviations, basis, sensitivity, blade_ids):
    total = deviations.shape[0] * lax.axis_size("pts") * lax.axis_size("blk")
    blades = deviations.shape[1]
    dims = (((0,), (0,)), ((), ()))
    term = lax.dot_general(deviations, deviations, dims, preferred_element_type=F32) / total
    row_part = lax.psum_scatter(term, "pts", scatter_dimension=0, tiled=True)
    gram = lax.psum_scatter(row_part, "blk", scatter_dimension=1, tiled=True)
    coeff_part = lax.dot_general(basis, deviations, dims, preferred_element_type=F32)
    energy_part = jnp.sum(jnp.square(deviations.astype(F32)), axis=0) / total
    selector = (jnp.arange(blades, dtype=jnp.int32)[:, None] == blade_ids[None, :]).astype(F32)
    coeffs, energy = lax.psum((coeff_part, energy_part), ("pts", "blk"))
    picked = jnp.dot(coeffs, selector, precision=lax.Precision.HIGHEST)
    picked_energy = jnp.dot(energy, selector, precision=lax.Precision.HIGHEST)
    weights = picked / jnp.sqrt(picked_energy + EPS)
    tiles = lax.all_to_all(sensitivity, "pts", split_axis=2, concat_axis=0, tiled=True)
    change = jnp.einsum("kb,kij->bij", weights, tiles.astype(F32), precision=lax.Precision.HIGHEST)
    return gram, change


def on_device(deviations, basis, sensitivity, blade_ids):
    count, cores = lax.axis_size("pts"), lax.axis_size("blk")
    points, blades = deviations.shape
    own, rows, order = sensitivity.shape
    outer, inner = split_of(count)
    fits = (
        cores == 2
        and outer * inner == count
        and outer % 2 == 0
        and (order // count) % GROUP == 0
        and (blades // count) % 8 == 0
        and (blades // cores) == 2 * basis.shape[1]
        and (blades // cores) % 128 == 0
        and rows % 128 == 0
        and order % 256 == 0
        and (inner * own * GROUP) % 128 == 0
        and points % (12 * 128) == 0
        and blade_ids.shape[0] % 8 == 0
    )
    run = in_kernel if fits else with_collectives
    return run(deviations, basis, sensitivity, blade_ids)


def solution(mesh):
    in_specs = (P(("pts", "blk"), None), P(("pts", "blk"), None), P("pts", "blk", None), P())
    out_specs = (P("pts", "blk"), P(None, "blk", "pts"))
    return jax.shard_map(
        on_device, mesh=mesh, in_specs=in_specs, out_specs=out_specs, check_vma=False
    )
```

```python
import functools

import jax
import jax.numpy as jnp
from jax import lax
from jax.experimental import pallas as pl
from jax.experimental.pallas import tpu as pltpu
from jax.sharding import PartitionSpec as P

MESH = pl.DeviceIdType.MESH
F32 = jnp.float32
BF16 = jnp.bfloat16
GROUP = 16
EPS = 1e-05


def split_of(count):
    inner = 1
    while inner * inner < count:
        inner *= 2
    return count // inner, inner


def kernel(
    dims, ids_hbm, dev_hbm, basis_hbm, sens_hbm, gram_ref, change_ref,
    ids_ref, dev_v, basis_v, sens_v, turned, blocks, gram_acc, coef_acc, spread_v, keep_v, w_hi, w_lo,
    s1, r1, s2, r2, s3, r3,
    ids_sem, dev_sem, basis_sem, sens_sem, own_sem, a_send, a_recv, c_send, c_recv, x_send, x_recv, z_send, z_recv,
):
    outer, inner, chunks, total = dims
    count = outer * inner
    half = outer // 2
    me = lax.axis_index("pts")
    core = lax.axis_index("blk")
    o, i = me // inner, me % inner
    side = o // half
    reals = ids_ref.shape[1]
    points, blades = dev_hbm.shape
    shapes = basis_hbm.shape[0]
    own, rows, order = sens_hbm.shape
    cols = order // count
    part = points // chunks
    gram_rows, gram_cols = gram_ref.shape
    span = order // 2

    barrier = pltpu.get_barrier_semaphore()
    for d in range(1, count):
        pl.semaphore_signal(barrier, inc=1, device_id=((me + d) % count, core), device_id_type=MESH)
    pl.semaphore_signal(barrier, inc=1, device_id=(me, 1 - core), device_id_type=MESH)

    far = pl.multiple_of((1 - side) * span, 128)
    near = pl.multiple_of(side * span, 128)
    loads = []
    for at, start in enumerate((far, near)):
        loads.append(
            pltpu.make_async_copy(
                sens_hbm.at[:, :, pl.ds(start, span)], sens_v.at[:, :, pl.ds(start, span)], sens_sem.at[at]
            )
        )
        loads[-1].start()
    ids_load = pltpu.make_async_copy(ids_hbm, ids_ref, ids_sem)
    ids_load.start()
    basis_load = pltpu.make_async_copy(basis_hbm, basis_v, basis_sem)
    basis_load.start()

    def dev_load(c):
        at = pl.ds(pl.multiple_of(c * part, part), part)
        return pltpu.make_async_copy(dev_hbm.at[at], dev_v.at[at], dev_sem.at[c])

    for c in range(chunks):
        dev_load(c).start()

    def turn(start):
        for k in range(own):
            turned[k, pl.ds(start, span), :] = sens_v[k, :, pl.ds(start, span)].T

    def block_to(peer):
        at = pl.ds(pl.multiple_of(peer * cols, cols), cols)
        return pltpu.make_async_remote_copy(
            src_ref=turned.at[:, at, :], dst_ref=blocks.at[me], send_sem=a_send.at[peer], recv_sem=a_recv.at[me],
            device_id=(peer, core), device_id_type=MESH,
        )

    def block_from(peer):
        return pltpu.make_async_remote_copy(
            src_ref=turned.at[:, pl.ds(0, cols), :], dst_ref=blocks.at[peer], send_sem=a_send.at[peer],
            recv_sem=a_recv.at[peer], device_id=(peer, core), device_id_type=MESH,
        )

    far_planes = [(1 - side) * half + (o + e) % half for e in range(half)]
    near_planes = [side * half + (o + e) % half for e in range(half)]

    loads[0].wait()
    turn(far)
    pl.semaphore_wait(barrier, count)
    sent = []
    crossing = [block_to(plane * inner + (i + e) % inner) for plane in far_planes for e in range(inner)]
    held = inner // 2
    for copy in crossing[:-held]:
        copy.start()
    loads[1].wait()
    turn(near)
    for at, plane in reversed(list(enumerate(near_planes))):
        for e in range(inner):
            if at == 0 and e == 0:
                continue
            sent.append(block_to(plane * inner + (i + e) % inner))
            sent[-1].start()
    mine = pltpu.make_async_copy(
        turned.at[:, pl.ds(pl.multiple_of(me * cols, cols), cols), :], blocks.at[me], own_sem
    )
    mine.start()

    spread_v[...] = (
        lax.broadcasted_iota(jnp.int32, spread_v.shape, 1) // GROUP == lax.broadcasted_iota(jnp.int32, spread_v.shape, 0)
    ).astype(F32).astype(BF16)
    keep_v[...] = (
        lax.broadcasted_iota(jnp.int32, keep_v.shape, 0) % GROUP
        == lax.broadcasted_iota(jnp.int32, keep_v.shape, 1) % GROUP
    ).astype(F32).astype(BF16)

    gram_acc[...] = jnp.zeros_like(gram_acc)
    coef_acc[...] = jnp.zeros_like(coef_acc)
    basis_load.wait()

    def accumulate(c, carry):
        dev_load(c).wait()
        start = pl.multiple_of(c * part, part)
        block = dev_v[pl.ds(start, part), :]
        gram_acc[...] += jnp.dot(block.T, block, preferred_element_type=F32)
        coef_acc[0:shapes, :] += jnp.dot(basis_v[:, pl.ds(start, part)], block, preferred_element_type=F32)
        return carry

    lax.fori_loop(0, chunks, accumulate, 0)

    wide = coef_acc.shape[0]
    ids_load.wait()
    ids = jnp.broadcast_to(ids_ref[...].astype(F32), (reals, reals))
    square = lax.broadcasted_iota(jnp.int32, (reals, reals), 0) == lax.broadcasted_iota(jnp.int32, (reals, reals), 1)
    ids_col = jnp.sum(jnp.where(square, ids, 0.0), axis=1, keepdims=True)
    lane = lax.broadcasted_iota(jnp.int32, (reals, blades), 1).astype(F32)
    chosen = jnp.where(ids_col == lane, 1.0, 0.0).astype(F32)
    gram = gram_acc[...]
    diagonal = lax.broadcasted_iota(jnp.int32, gram.shape, 0) == lax.broadcasted_iota(jnp.int32, gram.shape, 1)
    squares = jnp.sum(jnp.where(diagonal, gram, 0.0), axis=0, keepdims=True)
    energy = jnp.sum(chosen * squares, axis=1, keepdims=True)
    picked = lax.dot_general(
        chosen, coef_acc[...], (((1,), (1,)), ((), ())), preferred_element_type=F32, precision=lax.Precision.HIGHEST
    )
    place = lax.broadcasted_iota(jnp.int32, (reals, wide), 1)
    picked = jnp.where(place < shapes, picked, energy)

    for h in range(2):
        s1[h, 0:blades, :] = gram[:, h * gram_cols:(h + 1) * gram_cols]
        s1[h, blades:blades + reals, :] = picked
    over = pltpu.make_async_remote_copy(
        src_ref=s1.at[1 - core], dst_ref=r1, send_sem=c_send, recv_sem=c_recv,
        device_id=(me, 1 - core), device_id_type=MESH,
    )
    over.start()
    over.wait_recv()

    body = outer * gram_rows
    tail = s1[core, blades:blades + reals, :] + r1[blades:blades + reals, :]
    for j in range(inner):
        for q in range(outer):
            at = (q * inner + j) * gram_rows
            s2[j, q * gram_rows:(q + 1) * gram_rows, :] = (
                s1[core, at:at + gram_rows, :] + r1[at:at + gram_rows, :]
            )
        s2[j, body:body + reals, :] = tail
    plane_sent = []
    for e in range(1, inner):
        j = (i + e) % inner
        plane_sent.append(
            pltpu.make_async_remote_copy(
                src_ref=s2.at[j], dst_ref=r2.at[i], send_sem=x_send.at[j], recv_sem=x_recv.at[i],
                device_id=(o * inner + j, core), device_id_type=MESH,
            )
        )
        plane_sent[-1].start()
    value = s2[i]
    for e in range(1, inner):
        j = (i + e) % inner
        pltpu.make_async_remote_copy(
            src_ref=s2.at[j], dst_ref=r2.at[j], send_sem=x_send.at[j], recv_sem=x_recv.at[j],
            device_id=(o * inner + j, core), device_id_type=MESH,
        ).wait_recv()
        value = value + r2[j]

    for q in range(outer):
        s3[q, 0:gram_rows, :] = value[q * gram_rows:(q + 1) * gram_rows, :]
        s3[q, gram_rows:gram_rows + reals, :] = value[body:body + reals, :]
    out_sent = []
    for e in range(1, outer):
        q = (o + e) % outer
        out_sent.append(
            pltpu.make_async_remote_copy(
                src_ref=s3.at[q], dst_ref=r3.at[o], send_sem=z_send.at[q], recv_sem=z_recv.at[o],
                device_id=(q * inner + i, core), device_id_type=MESH,
            )
        )
        out_sent[-1].start()
    for copy in crossing[-held:]:
        copy.start()
    value = s3[o]
    for e in range(1, outer):
        q = (o + e) % outer
        pltpu.make_async_remote_copy(
            src_ref=s3.at[q], dst_ref=r3.at[q], send_sem=z_send.at[q], recv_sem=z_recv.at[q],
            device_id=(q * inner + i, core), device_id_type=MESH,
        ).wait_recv()
        value = value + r3[q]
    gram_ref[...] = value[0:gram_rows, :] / total

    packed = value[gram_rows:gram_rows + reals, :]
    moved = pltpu.roll(packed, wide - shapes, 1)
    weights = jnp.where(place < shapes, packed / jnp.sqrt(jnp.where(place < shapes, moved, 0.0) / total + EPS), 0.0)
    tall = jnp.broadcast_to(weights[:, None, :], (reals, GROUP, wide)).reshape(reals * GROUP, wide)
    hi = tall.astype(BF16)
    lo = (tall - hi.astype(F32)).astype(BF16)
    spread = spread_v[...]
    w_hi[...] = jnp.dot(hi, spread, preferred_element_type=F32).astype(BF16) * keep_v[...]
    w_lo[...] = jnp.dot(lo, spread, preferred_element_type=F32).astype(BF16) * keep_v[...]

    mine.wait()
    step = inner * own * GROUP
    for at, plane in enumerate(near_planes + far_planes):
        for e in range(inner):
            if at == 0 and e == 0:
                continue
            block_from(plane * inner + (i + e) % inner).wait_recv()
        lanes = pl.ds(pl.multiple_of(plane * step, step), step)
        left_hi, left_lo = w_hi[:, lanes], w_lo[:, lanes]
        for g in range(cols // GROUP):
            here = slice(g * GROUP, (g + 1) * GROUP)
            right = blocks[pl.ds(plane * inner, inner), :, here, :].reshape(step, rows)
            term = jnp.dot(left_hi, right, preferred_element_type=F32) + jnp.dot(
                left_lo, right, preferred_element_type=F32
            )
            term = term.reshape(reals, GROUP, rows)
            if at == 0:
                change_ref[:, here, :] = term
            else:
                change_ref[:, here, :] += term

    over.wait_send()
    for copy in crossing + sent + plane_sent + out_sent:
        copy.wait_send()


def hand_over(pieces, gram_ref, change_ref, gram_out, change_out, sems):
    part = change_ref.shape[0] // pieces
    copies = [pltpu.make_async_copy(gram_ref, gram_out, sems.at[pieces])]
    for at in range(pieces):
        here = pl.ds(at * part, part)
        copies.append(pltpu.make_async_copy(change_ref.at[here], change_out.at[here], sems.at[at]))
    for copy in copies:
        copy.start()
    for copy in copies:
        copy.wait()


def in_kernel(deviations, basis, sensitivity, blade_ids):
    count = lax.axis_size("pts")
    cores = lax.axis_size("blk")
    points, blades = deviations.shape
    shapes = basis.shape[1]
    own, rows, order = sensitivity.shape
    reals = blade_ids.shape[0]
    outer, inner = split_of(count)
    cols = order // count
    gram_rows, gram_cols = blades // count, blades // cores
    chunks = 12
    wide = 2 * shapes
    total = float(points * count * cores)
    hbm = pl.BlockSpec(memory_space=pltpu.HBM)
    vmem = pl.BlockSpec(memory_space=pltpu.VMEM)
    sem = pltpu.SemaphoreType.DMA
    body = outer * gram_rows
    flops = 2 * points * blades * (blades + shapes) + 4 * reals * shapes * GROUP * rows * cols
    gram, change = pl.pallas_call(
        functools.partial(kernel, (outer, inner, chunks, total)),
        out_shape=(pltpu.VMEM((gram_rows, gram_cols), F32), pltpu.VMEM((reals, cols, rows), F32)),
        in_specs=[hbm, hbm, hbm, hbm],
        out_specs=(vmem, vmem),
        scratch_shapes=[
            pltpu.VMEM((1, reals), jnp.int32),
            pltpu.VMEM((points, blades), BF16),
            pltpu.VMEM((shapes, points), BF16),
            pltpu.VMEM((own, rows, order), BF16),
            pltpu.VMEM((own, order, rows), BF16),
            pltpu.VMEM((count, own, cols, rows), BF16),
            pltpu.VMEM((blades, blades), F32),
            pltpu.VMEM((wide, blades), F32),
            pltpu.VMEM((wide, shapes * GROUP), BF16),
            pltpu.VMEM((reals * GROUP, shapes * GROUP), BF16),
            pltpu.VMEM((reals * GROUP, shapes * GROUP), BF16),
            pltpu.VMEM((reals * GROUP, shapes * GROUP), BF16),
            pltpu.VMEM((2, blades + reals, gram_cols), F32),
            pltpu.VMEM((blades + reals, gram_cols), F32),
            pltpu.VMEM((inner, body + reals, gram_cols), F32),
            pltpu.VMEM((inner, body + reals, gram_cols), F32),
            pltpu.VMEM((outer, gram_rows + reals, gram_cols), F32),
            pltpu.VMEM((outer, gram_rows + reals, gram_cols), F32),
            sem, sem((chunks,)), sem, sem((2,)), sem,
            sem((count,)), sem((count,)), sem, sem,
            sem((inner,)), sem((inner,)), sem((outer,)), sem((outer,)),
        ],
        compiler_params=pltpu.CompilerParams(
            collective_id=0, has_side_effects=True, vmem_limit_bytes=32 * 1024 * 1024
        ),
        cost_estimate=pl.CostEstimate(
            flops=flops, transcendentals=0, bytes_accessed=2 * points * (blades + shapes) + 8 * own * rows * order
        ),
    )(
        pltpu.with_memory_space_constraint(blade_ids[None, :], pltpu.HBM),
        pltpu.with_memory_space_constraint(deviations, pltpu.HBM),
        pltpu.with_memory_space_constraint(basis.T, pltpu.HBM),
        pltpu.with_memory_space_constraint(sensitivity, pltpu.HBM),
    )
    pieces = 4
    gram, change = pl.pallas_call(
        functools.partial(hand_over, pieces),
        out_shape=(
            jax.ShapeDtypeStruct((gram_rows, gram_cols), F32),
            jax.ShapeDtypeStruct((reals, cols, rows), F32),
        ),
        in_specs=[vmem, vmem],
        out_specs=(hbm, hbm),
        scratch_shapes=[sem((pieces + 1,))],
        compiler_params=pltpu.CompilerParams(vmem_limit_bytes=4 * 1024 * 1024),
    )(
        pltpu.with_memory_space_constraint(gram, pltpu.VMEM),
        pltpu.with_memory_space_constraint(change, pltpu.VMEM),
    )
    return gram, jnp.transpose(change, (0, 2, 1))


def with_collectives(deviations, basis, sensitivity, blade_ids):
    total = deviations.shape[0] * lax.axis_size("pts") * lax.axis_size("blk")
    blades = deviations.shape[1]
    dims = (((0,), (0,)), ((), ()))
    term = lax.dot_general(deviations, deviations, dims, preferred_element_type=F32) / total
    row_part = lax.psum_scatter(term, "pts", scatter_dimension=0, tiled=True)
    gram = lax.psum_scatter(row_part, "blk", scatter_dimension=1, tiled=True)
    coeff_part = lax.dot_general(basis, deviations, dims, preferred_element_type=F32)
    energy_part = jnp.sum(jnp.square(deviations.astype(F32)), axis=0) / total
    selector = (jnp.arange(blades, dtype=jnp.int32)[:, None] == blade_ids[None, :]).astype(F32)
    coeffs, energy = lax.psum((coeff_part, energy_part), ("pts", "blk"))
    picked = jnp.dot(coeffs, selector, precision=lax.Precision.HIGHEST)
    picked_energy = jnp.dot(energy, selector, precision=lax.Precision.HIGHEST)
    weights = picked / jnp.sqrt(picked_energy + EPS)
    tiles = lax.all_to_all(sensitivity, "pts", split_axis=2, concat_axis=0, tiled=True)
    change = jnp.einsum("kb,kij->bij", weights, tiles.astype(F32), precision=lax.Precision.HIGHEST)
    return gram, change


def on_device(deviations, basis, sensitivity, blade_ids):
    count, cores = lax.axis_size("pts"), lax.axis_size("blk")
    points, blades = deviations.shape
    own, rows, order = sensitivity.shape
    outer, inner = split_of(count)
    fits = (
        cores == 2
        and outer * inner == count
        and outer % 2 == 0
        and (order // count) % GROUP == 0
        and (blades // count) % 8 == 0
        and (blades // cores) == 2 * basis.shape[1]
        and (blades // cores) % 128 == 0
        and rows % 128 == 0
        and order % 256 == 0
        and (inner * own * GROUP) % 128 == 0
        and points % (12 * 128) == 0
        and blade_ids.shape[0] % 8 == 0
    )
    run = in_kernel if fits else with_collectives
    return run(deviations, basis, sensitivity, blade_ids)


def solution(mesh):
    in_specs = (P(("pts", "blk"), None), P(("pts", "blk"), None), P("pts", "blk", None), P())
    out_specs = (P("pts", "blk"), P(None, "blk", "pts"))
    return jax.shard_map(
        on_device, mesh=mesh, in_specs=in_specs, out_specs=out_specs, check_vma=False
    )
```

```python
import functools

import jax
import jax.numpy as jnp
from jax import lax
from jax.experimental import pallas as pl
from jax.experimental.pallas import tpu as pltpu
from jax.sharding import PartitionSpec as P

MESH = pl.DeviceIdType.MESH
F32 = jnp.float32
BF16 = jnp.bfloat16
GROUP = 16
EPS = 1e-05


def split_of(count):
    inner = 1
    while inner * inner < count:
        inner *= 2
    return count // inner, inner


def kernel(
    dims, ids_hbm, dev_hbm, basis_hbm, sens_hbm, gram_ref, change_ref,
    ids_ref, dev_v, basis_v, sens_v, turned, blocks, gram_acc, coef_acc, spread_v, keep_v, w_hi, w_lo,
    s1, r1, s2, r2, s3, r3,
    ids_sem, dev_sem, basis_sem, sens_sem, own_sem, a_send, a_recv, c_send, c_recv, x_send, x_recv, z_send, z_recv,
):
    outer, inner, chunks, total = dims
    count = outer * inner
    half = outer // 2
    me = lax.axis_index("pts")
    core = lax.axis_index("blk")
    o, i = me // inner, me % inner
    side = o // half
    reals = ids_ref.shape[1]
    points, blades = dev_hbm.shape
    shapes = basis_hbm.shape[0]
    own, rows, order = sens_hbm.shape
    cols = order // count
    part = points // chunks
    gram_rows, gram_cols = gram_ref.shape
    span = cols * inner

    barrier = pltpu.get_barrier_semaphore()
    for d in range(1, count):
        pl.semaphore_signal(barrier, inc=1, device_id=((me + d) % count, core), device_id_type=MESH)
    pl.semaphore_signal(barrier, inc=1, device_id=(me, 1 - core), device_id_type=MESH)

    far_planes = [(1 - side) * half + (o + e) % half for e in range(half)]
    near_planes = [side * half + (o + e) % half for e in range(half)]
    loads = []
    for at, plane in enumerate(far_planes + near_planes):
        here = pl.ds(pl.multiple_of(plane * span, span), span)
        loads.append(pltpu.make_async_copy(sens_hbm.at[:, :, here], sens_v.at[:, :, here], sens_sem.at[at]))
        loads[-1].start()
    ids_load = pltpu.make_async_copy(ids_hbm, ids_ref, ids_sem)
    ids_load.start()
    basis_load = pltpu.make_async_copy(basis_hbm, basis_v, basis_sem)
    basis_load.start()

    def dev_load(c):
        at = pl.ds(pl.multiple_of(c * part, part), part)
        return pltpu.make_async_copy(dev_hbm.at[at], dev_v.at[at], dev_sem.at[c])

    for c in range(chunks):
        dev_load(c).start()

    def turn(plane):
        here = pl.ds(pl.multiple_of(plane * span, span), span)
        for k in range(own):
            turned[k, here, :] = sens_v[k, :, here].T

    def block_to(peer):
        at = pl.ds(pl.multiple_of(peer * cols, cols), cols)
        return pltpu.make_async_remote_copy(
            src_ref=turned.at[:, at, :], dst_ref=blocks.at[me], send_sem=a_send.at[peer], recv_sem=a_recv.at[me],
            device_id=(peer, core), device_id_type=MESH,
        )

    def block_from(peer):
        return pltpu.make_async_remote_copy(
            src_ref=turned.at[:, pl.ds(0, cols), :], dst_ref=blocks.at[peer], send_sem=a_send.at[peer],
            recv_sem=a_recv.at[peer], device_id=(peer, core), device_id_type=MESH,
        )

    crossing = [block_to(plane * inner + (i + e) % inner) for plane in far_planes for e in range(inner)]
    early = len(crossing) - inner
    for at, plane in enumerate(far_planes):
        loads[at].wait()
        turn(plane)
        if at == 0:
            pl.semaphore_wait(barrier, count)
        for copy in crossing[at * inner:min((at + 1) * inner, early)]:
            copy.start()
    sent = []
    for at, plane in reversed(list(enumerate(near_planes))):
        loads[half + at].wait()
        turn(plane)
        for e in range(inner):
            if at == 0 and e == 0:
                continue
            sent.append(block_to(plane * inner + (i + e) % inner))
            sent[-1].start()
    mine = pltpu.make_async_copy(
        turned.at[:, pl.ds(pl.multiple_of(me * cols, cols), cols), :], blocks.at[me], own_sem
    )
    mine.start()

    spread_v[...] = (
        lax.broadcasted_iota(jnp.int32, spread_v.shape, 1) // GROUP == lax.broadcasted_iota(jnp.int32, spread_v.shape, 0)
    ).astype(F32).astype(BF16)
    keep_v[...] = (
        lax.broadcasted_iota(jnp.int32, keep_v.shape, 0) % GROUP
        == lax.broadcasted_iota(jnp.int32, keep_v.shape, 1) % GROUP
    ).astype(F32).astype(BF16)

    gram_acc[...] = jnp.zeros_like(gram_acc)
    coef_acc[...] = jnp.zeros_like(coef_acc)
    basis_load.wait()

    def accumulate(c, carry):
        dev_load(c).wait()
        start = pl.multiple_of(c * part, part)
        block = dev_v[pl.ds(start, part), :]
        gram_acc[...] += jnp.dot(block.T, block, preferred_element_type=F32)
        coef_acc[0:shapes, :] += jnp.dot(basis_v[:, pl.ds(start, part)], block, preferred_element_type=F32)
        return carry

    lax.fori_loop(0, chunks, accumulate, 0)

    wide = coef_acc.shape[0]
    ids_load.wait()
    ids = jnp.broadcast_to(ids_ref[...].astype(F32), (reals, reals))
    square = lax.broadcasted_iota(jnp.int32, (reals, reals), 0) == lax.broadcasted_iota(jnp.int32, (reals, reals), 1)
    ids_col = jnp.sum(jnp.where(square, ids, 0.0), axis=1, keepdims=True)
    lane = lax.broadcasted_iota(jnp.int32, (reals, blades), 1).astype(F32)
    chosen = jnp.where(ids_col == lane, 1.0, 0.0).astype(F32)
    gram = gram_acc[...]
    diagonal = lax.broadcasted_iota(jnp.int32, gram.shape, 0) == lax.broadcasted_iota(jnp.int32, gram.shape, 1)
    squares = jnp.sum(jnp.where(diagonal, gram, 0.0), axis=0, keepdims=True)
    energy = jnp.sum(chosen * squares, axis=1, keepdims=True)
    picked = lax.dot_general(
        chosen, coef_acc[...], (((1,), (1,)), ((), ())), preferred_element_type=F32, precision=lax.Precision.HIGHEST
    )
    place = lax.broadcasted_iota(jnp.int32, (reals, wide), 1)
    picked = jnp.where(place < shapes, picked, energy)

    for h in range(2):
        s1[h, 0:blades, :] = gram[:, h * gram_cols:(h + 1) * gram_cols]
        s1[h, blades:blades + reals, :] = picked
    over = pltpu.make_async_remote_copy(
        src_ref=s1.at[1 - core], dst_ref=r1, send_sem=c_send, recv_sem=c_recv,
        device_id=(me, 1 - core), device_id_type=MESH,
    )
    over.start()
    over.wait_recv()

    body = outer * gram_rows
    tail = s1[core, blades:blades + reals, :] + r1[blades:blades + reals, :]
    for j in range(inner):
        for q in range(outer):
            at = (q * inner + j) * gram_rows
            s2[j, q * gram_rows:(q + 1) * gram_rows, :] = (
                s1[core, at:at + gram_rows, :] + r1[at:at + gram_rows, :]
            )
        s2[j, body:body + reals, :] = tail
    plane_sent = []
    for e in range(1, inner):
        j = (i + e) % inner
        plane_sent.append(
            pltpu.make_async_remote_copy(
                src_ref=s2.at[j], dst_ref=r2.at[i], send_sem=x_send.at[j], recv_sem=x_recv.at[i],
                device_id=(o * inner + j, core), device_id_type=MESH,
            )
        )
        plane_sent[-1].start()
    value = s2[i]
    for e in range(1, inner):
        j = (i + e) % inner
        pltpu.make_async_remote_copy(
            src_ref=s2.at[j], dst_ref=r2.at[j], send_sem=x_send.at[j], recv_sem=x_recv.at[j],
            device_id=(o * inner + j, core), device_id_type=MESH,
        ).wait_recv()
        value = value + r2[j]

    for q in range(outer):
        s3[q, 0:gram_rows, :] = value[q * gram_rows:(q + 1) * gram_rows, :]
        s3[q, gram_rows:gram_rows + reals, :] = value[body:body + reals, :]
    out_sent = []
    for e in range(1, outer):
        q = (o + e) % outer
        out_sent.append(
            pltpu.make_async_remote_copy(
                src_ref=s3.at[q], dst_ref=r3.at[o], send_sem=z_send.at[q], recv_sem=z_recv.at[o],
                device_id=(q * inner + i, core), device_id_type=MESH,
            )
        )
        out_sent[-1].start()
    for copy in crossing[early:]:
        copy.start()
    value = s3[o]
    for e in range(1, outer):
        q = (o + e) % outer
        pltpu.make_async_remote_copy(
            src_ref=s3.at[q], dst_ref=r3.at[q], send_sem=z_send.at[q], recv_sem=z_recv.at[q],
            device_id=(q * inner + i, core), device_id_type=MESH,
        ).wait_recv()
        value = value + r3[q]
    gram_ref[...] = value[0:gram_rows, :] / total

    packed = value[gram_rows:gram_rows + reals, :]
    moved = pltpu.roll(packed, wide - shapes, 1)
    weights = jnp.where(place < shapes, packed / jnp.sqrt(jnp.where(place < shapes, moved, 0.0) / total + EPS), 0.0)
    tall = jnp.broadcast_to(weights[:, None, :], (reals, GROUP, wide)).reshape(reals * GROUP, wide)
    hi = tall.astype(BF16)
    lo = (tall - hi.astype(F32)).astype(BF16)
    spread = spread_v[...]
    w_hi[...] = jnp.dot(hi, spread, preferred_element_type=F32).astype(BF16) * keep_v[...]
    w_lo[...] = jnp.dot(lo, spread, preferred_element_type=F32).astype(BF16) * keep_v[...]

    mine.wait()
    step = inner * own * GROUP
    for at, plane in enumerate(near_planes + far_planes):
        for e in range(inner):
            if at == 0 and e == 0:
                continue
            block_from(plane * inner + (i + e) % inner).wait_recv()
        lanes = pl.ds(pl.multiple_of(plane * step, step), step)
        left_hi, left_lo = w_hi[:, lanes], w_lo[:, lanes]
        for g in range(cols // GROUP):
            here = slice(g * GROUP, (g + 1) * GROUP)
            right = blocks[pl.ds(plane * inner, inner), :, here, :].reshape(step, rows)
            term = jnp.dot(left_hi, right, preferred_element_type=F32) + jnp.dot(
                left_lo, right, preferred_element_type=F32
            )
            term = term.reshape(reals, GROUP, rows)
            if at == 0:
                change_ref[:, here, :] = term
            else:
                change_ref[:, here, :] += term

    over.wait_send()
    for copy in crossing + sent + plane_sent + out_sent:
        copy.wait_send()


def hand_over(pieces, gram_ref, change_ref, gram_out, change_out, sems):
    part = change_ref.shape[0] // pieces
    copies = [pltpu.make_async_copy(gram_ref, gram_out, sems.at[pieces])]
    for at in range(pieces):
        here = pl.ds(at * part, part)
        copies.append(pltpu.make_async_copy(change_ref.at[here], change_out.at[here], sems.at[at]))
    for copy in copies:
        copy.start()
    for copy in copies:
        copy.wait()


def in_kernel(deviations, basis, sensitivity, blade_ids):
    count = lax.axis_size("pts")
    cores = lax.axis_size("blk")
    points, blades = deviations.shape
    shapes = basis.shape[1]
    own, rows, order = sensitivity.shape
    reals = blade_ids.shape[0]
    outer, inner = split_of(count)
    cols = order // count
    gram_rows, gram_cols = blades // count, blades // cores
    chunks = 12
    wide = 2 * shapes
    total = float(points * count * cores)
    hbm = pl.BlockSpec(memory_space=pltpu.HBM)
    vmem = pl.BlockSpec(memory_space=pltpu.VMEM)
    sem = pltpu.SemaphoreType.DMA
    body = outer * gram_rows
    flops = 2 * points * blades * (blades + shapes) + 4 * reals * shapes * GROUP * rows * cols
    gram, change = pl.pallas_call(
        functools.partial(kernel, (outer, inner, chunks, total)),
        out_shape=(pltpu.VMEM((gram_rows, gram_cols), F32), pltpu.VMEM((reals, cols, rows), F32)),
        in_specs=[hbm, hbm, hbm, hbm],
        out_specs=(vmem, vmem),
        scratch_shapes=[
            pltpu.VMEM((1, reals), jnp.int32),
            pltpu.VMEM((points, blades), BF16),
            pltpu.VMEM((shapes, points), BF16),
            pltpu.VMEM((own, rows, order), BF16),
            pltpu.VMEM((own, order, rows), BF16),
            pltpu.VMEM((count, own, cols, rows), BF16),
            pltpu.VMEM((blades, blades), F32),
            pltpu.VMEM((wide, blades), F32),
            pltpu.VMEM((wide, shapes * GROUP), BF16),
            pltpu.VMEM((reals * GROUP, shapes * GROUP), BF16),
            pltpu.VMEM((reals * GROUP, shapes * GROUP), BF16),
            pltpu.VMEM((reals * GROUP, shapes * GROUP), BF16),
            pltpu.VMEM((2, blades + reals, gram_cols), F32),
            pltpu.VMEM((blades + reals, gram_cols), F32),
            pltpu.VMEM((inner, body + reals, gram_cols), F32),
            pltpu.VMEM((inner, body + reals, gram_cols), F32),
            pltpu.VMEM((outer, gram_rows + reals, gram_cols), F32),
            pltpu.VMEM((outer, gram_rows + reals, gram_cols), F32),
            sem, sem((chunks,)), sem, sem((outer,)), sem,
            sem((count,)), sem((count,)), sem, sem,
            sem((inner,)), sem((inner,)), sem((outer,)), sem((outer,)),
        ],
        compiler_params=pltpu.CompilerParams(
            collective_id=0, has_side_effects=True, vmem_limit_bytes=32 * 1024 * 1024
        ),
        cost_estimate=pl.CostEstimate(
            flops=flops, transcendentals=0, bytes_accessed=2 * points * (blades + shapes) + 8 * own * rows * order
        ),
    )(
        pltpu.with_memory_space_constraint(blade_ids[None, :], pltpu.HBM),
        pltpu.with_memory_space_constraint(deviations, pltpu.HBM),
        pltpu.with_memory_space_constraint(basis.T, pltpu.HBM),
        pltpu.with_memory_space_constraint(sensitivity, pltpu.HBM),
    )
    pieces = 4
    gram, change = pl.pallas_call(
        functools.partial(hand_over, pieces),
        out_shape=(
            jax.ShapeDtypeStruct((gram_rows, gram_cols), F32),
            jax.ShapeDtypeStruct((reals, cols, rows), F32),
        ),
        in_specs=[vmem, vmem],
        out_specs=(hbm, hbm),
        scratch_shapes=[sem((pieces + 1,))],
        compiler_params=pltpu.CompilerParams(vmem_limit_bytes=4 * 1024 * 1024),
    )(
        pltpu.with_memory_space_constraint(gram, pltpu.VMEM),
        pltpu.with_memory_space_constraint(change, pltpu.VMEM),
    )
    return gram, jnp.transpose(change, (0, 2, 1))


def with_collectives(deviations, basis, sensitivity, blade_ids):
    total = deviations.shape[0] * lax.axis_size("pts") * lax.axis_size("blk")
    blades = deviations.shape[1]
    dims = (((0,), (0,)), ((), ()))
    term = lax.dot_general(deviations, deviations, dims, preferred_element_type=F32) / total
    row_part = lax.psum_scatter(term, "pts", scatter_dimension=0, tiled=True)
    gram = lax.psum_scatter(row_part, "blk", scatter_dimension=1, tiled=True)
    coeff_part = lax.dot_general(basis, deviations, dims, preferred_element_type=F32)
    energy_part = jnp.sum(jnp.square(deviations.astype(F32)), axis=0) / total
    selector = (jnp.arange(blades, dtype=jnp.int32)[:, None] == blade_ids[None, :]).astype(F32)
    coeffs, energy = lax.psum((coeff_part, energy_part), ("pts", "blk"))
    picked = jnp.dot(coeffs, selector, precision=lax.Precision.HIGHEST)
    picked_energy = jnp.dot(energy, selector, precision=lax.Precision.HIGHEST)
    weights = picked / jnp.sqrt(picked_energy + EPS)
    tiles = lax.all_to_all(sensitivity, "pts", split_axis=2, concat_axis=0, tiled=True)
    change = jnp.einsum("kb,kij->bij", weights, tiles.astype(F32), precision=lax.Precision.HIGHEST)
    return gram, change


def on_device(deviations, basis, sensitivity, blade_ids):
    count, cores = lax.axis_size("pts"), lax.axis_size("blk")
    points, blades = deviations.shape
    own, rows, order = sensitivity.shape
    outer, inner = split_of(count)
    fits = (
        cores == 2
        and outer * inner == count
        and outer % 2 == 0
        and (order // count) % GROUP == 0
        and (blades // count) % 8 == 0
        and (blades // cores) == 2 * basis.shape[1]
        and (blades // cores) % 128 == 0
        and rows % 128 == 0
        and (order // count * inner) % 128 == 0
        and (inner * own * GROUP) % 128 == 0
        and points % (12 * 128) == 0
        and blade_ids.shape[0] % 8 == 0
    )
    run = in_kernel if fits else with_collectives
    return run(deviations, basis, sensitivity, blade_ids)


def solution(mesh):
    in_specs = (P(("pts", "blk"), None), P(("pts", "blk"), None), P("pts", "blk", None), P())
    out_specs = (P("pts", "blk"), P(None, "blk", "pts"))
    return jax.shard_map(
        on_device, mesh=mesh, in_specs=in_specs, out_specs=out_specs, check_vma=False
    )
```

```python
import functools

import jax
import jax.numpy as jnp
from jax import lax
from jax.experimental import pallas as pl
from jax.experimental.pallas import tpu as pltpu
from jax.sharding import PartitionSpec as P

MESH = pl.DeviceIdType.MESH
F32 = jnp.float32
BF16 = jnp.bfloat16
GROUP = 16
EPS = 1e-05


def split_of(count):
    inner = 1
    while inner * inner < count:
        inner *= 2
    return count // inner, inner


def kernel(
    dims, ids_hbm, dev_hbm, basis_hbm, sens_hbm, gram_ref, change_ref,
    ids_ref, dev_v, basis_v, sens_v, turned, blocks, gram_acc, coef_acc, spread_v, keep_v, w_hi, w_lo,
    s1, r1, s2, r2, s3, r3,
    ids_sem, dev_sem, basis_sem, sens_sem, own_sem, a_send, a_recv, c_send, c_recv, x_send, x_recv, z_send, z_recv,
):
    outer, inner, chunks, total = dims
    count = outer * inner
    half = outer // 2
    me = lax.axis_index("pts")
    core = lax.axis_index("blk")
    o, i = me // inner, me % inner
    side = o // half
    reals = ids_ref.shape[1]
    points, blades = dev_hbm.shape
    shapes = basis_hbm.shape[0]
    own, rows, order = sens_hbm.shape
    cols = order // count
    part = points // chunks
    gram_rows, gram_cols = gram_ref.shape
    span = cols * inner

    barrier = pltpu.get_barrier_semaphore()
    for d in range(1, count):
        pl.semaphore_signal(barrier, inc=1, device_id=((me + d) % count, core), device_id_type=MESH)
    pl.semaphore_signal(barrier, inc=1, device_id=(me, 1 - core), device_id_type=MESH)

    far_planes = [(1 - side) * half + (o + e) % half for e in range(half)]
    near_planes = [side * half + (o + e) % half for e in range(half)]
    loads = []
    for at, plane in enumerate(far_planes + near_planes):
        here = pl.ds(pl.multiple_of(plane * span, span), span)
        loads.append(pltpu.make_async_copy(sens_hbm.at[:, :, here], sens_v.at[:, :, here], sens_sem.at[at]))
        loads[-1].start()
    ids_load = pltpu.make_async_copy(ids_hbm, ids_ref, ids_sem)
    ids_load.start()
    basis_load = pltpu.make_async_copy(basis_hbm, basis_v, basis_sem)
    basis_load.start()

    def dev_load(c):
        at = pl.ds(pl.multiple_of(c * part, part), part)
        return pltpu.make_async_copy(dev_hbm.at[at], dev_v.at[at], dev_sem.at[c])

    for c in range(chunks):
        dev_load(c).start()

    def turn(plane):
        here = pl.ds(pl.multiple_of(plane * span, span), span)
        for k in range(own):
            turned[k, here, :] = sens_v[k, :, here].T

    def block_to(peer):
        at = pl.ds(pl.multiple_of(peer * cols, cols), cols)
        return pltpu.make_async_remote_copy(
            src_ref=turned.at[:, at, :], dst_ref=blocks.at[me], send_sem=a_send.at[peer], recv_sem=a_recv.at[me],
            device_id=(peer, core), device_id_type=MESH,
        )

    def block_from(peer):
        return pltpu.make_async_remote_copy(
            src_ref=turned.at[:, pl.ds(0, cols), :], dst_ref=blocks.at[peer], send_sem=a_send.at[peer],
            recv_sem=a_recv.at[peer], device_id=(peer, core), device_id_type=MESH,
        )

    crossing = [block_to(plane * inner + (i + e) % inner) for plane in far_planes for e in range(inner)]
    early = len(crossing) - (inner - 1)
    for at, plane in enumerate(far_planes):
        loads[at].wait()
        turn(plane)
        if at == 0:
            pl.semaphore_wait(barrier, count)
        for copy in crossing[at * inner:min((at + 1) * inner, early)]:
            copy.start()
    sent = []
    for at, plane in reversed(list(enumerate(near_planes))):
        loads[half + at].wait()
        turn(plane)
        for e in range(inner):
            if at == 0 and e == 0:
                continue
            sent.append(block_to(plane * inner + (i + e) % inner))
    mine = pltpu.make_async_copy(
        turned.at[:, pl.ds(pl.multiple_of(me * cols, cols), cols), :], blocks.at[me], own_sem
    )
    mine.start()

    spread_v[...] = (
        lax.broadcasted_iota(jnp.int32, spread_v.shape, 1) // GROUP == lax.broadcasted_iota(jnp.int32, spread_v.shape, 0)
    ).astype(F32).astype(BF16)
    keep_v[...] = (
        lax.broadcasted_iota(jnp.int32, keep_v.shape, 0) % GROUP
        == lax.broadcasted_iota(jnp.int32, keep_v.shape, 1) % GROUP
    ).astype(F32).astype(BF16)

    gram_acc[...] = jnp.zeros_like(gram_acc)
    coef_acc[...] = jnp.zeros_like(coef_acc)
    basis_load.wait()

    def accumulate(c, carry):
        dev_load(c).wait()
        start = pl.multiple_of(c * part, part)
        block = dev_v[pl.ds(start, part), :]
        gram_acc[...] += jnp.dot(block.T, block, preferred_element_type=F32)
        coef_acc[0:shapes, :] += jnp.dot(basis_v[:, pl.ds(start, part)], block, preferred_element_type=F32)
        return carry

    lax.fori_loop(0, chunks, accumulate, 0)

    wide = coef_acc.shape[0]
    ids_load.wait()
    ids = jnp.broadcast_to(ids_ref[...].astype(F32), (reals, reals))
    square = lax.broadcasted_iota(jnp.int32, (reals, reals), 0) == lax.broadcasted_iota(jnp.int32, (reals, reals), 1)
    ids_col = jnp.sum(jnp.where(square, ids, 0.0), axis=1, keepdims=True)
    lane = lax.broadcasted_iota(jnp.int32, (reals, blades), 1).astype(F32)
    chosen = jnp.where(ids_col == lane, 1.0, 0.0).astype(F32)
    gram = gram_acc[...]
    diagonal = lax.broadcasted_iota(jnp.int32, gram.shape, 0) == lax.broadcasted_iota(jnp.int32, gram.shape, 1)
    squares = jnp.sum(jnp.where(diagonal, gram, 0.0), axis=0, keepdims=True)
    energy = jnp.sum(chosen * squares, axis=1, keepdims=True)
    picked = lax.dot_general(
        chosen, coef_acc[...], (((1,), (1,)), ((), ())), preferred_element_type=F32, precision=lax.Precision.HIGHEST
    )
    place = lax.broadcasted_iota(jnp.int32, (reals, wide), 1)
    picked = jnp.where(place < shapes, picked, energy)

    for h in range(2):
        s1[h, 0:blades, :] = gram[:, h * gram_cols:(h + 1) * gram_cols]
        s1[h, blades:blades + reals, :] = picked
    over = pltpu.make_async_remote_copy(
        src_ref=s1.at[1 - core], dst_ref=r1, send_sem=c_send, recv_sem=c_recv,
        device_id=(me, 1 - core), device_id_type=MESH,
    )
    over.start()
    over.wait_recv()

    body = outer * gram_rows
    tail = s1[core, blades:blades + reals, :] + r1[blades:blades + reals, :]
    for j in range(inner):
        for q in range(outer):
            at = (q * inner + j) * gram_rows
            s2[j, q * gram_rows:(q + 1) * gram_rows, :] = (
                s1[core, at:at + gram_rows, :] + r1[at:at + gram_rows, :]
            )
        s2[j, body:body + reals, :] = tail
    plane_sent = []
    for e in range(1, inner):
        j = (i + e) % inner
        plane_sent.append(
            pltpu.make_async_remote_copy(
                src_ref=s2.at[j], dst_ref=r2.at[i], send_sem=x_send.at[j], recv_sem=x_recv.at[i],
                device_id=(o * inner + j, core), device_id_type=MESH,
            )
        )
        plane_sent[-1].start()
    for copy in sent:
        copy.start()
    value = s2[i]
    for e in range(1, inner):
        j = (i + e) % inner
        pltpu.make_async_remote_copy(
            src_ref=s2.at[j], dst_ref=r2.at[j], send_sem=x_send.at[j], recv_sem=x_recv.at[j],
            device_id=(o * inner + j, core), device_id_type=MESH,
        ).wait_recv()
        value = value + r2[j]

    for q in range(outer):
        s3[q, 0:gram_rows, :] = value[q * gram_rows:(q + 1) * gram_rows, :]
        s3[q, gram_rows:gram_rows + reals, :] = value[body:body + reals, :]
    out_sent = []
    for e in range(1, outer):
        q = (o + e) % outer
        out_sent.append(
            pltpu.make_async_remote_copy(
                src_ref=s3.at[q], dst_ref=r3.at[o], send_sem=z_send.at[q], recv_sem=z_recv.at[o],
                device_id=(q * inner + i, core), device_id_type=MESH,
            )
        )
        out_sent[-1].start()
    for copy in crossing[early:]:
        copy.start()
    value = s3[o]
    for e in range(1, outer):
        q = (o + e) % outer
        pltpu.make_async_remote_copy(
            src_ref=s3.at[q], dst_ref=r3.at[q], send_sem=z_send.at[q], recv_sem=z_recv.at[q],
            device_id=(q * inner + i, core), device_id_type=MESH,
        ).wait_recv()
        value = value + r3[q]
    gram_ref[...] = value[0:gram_rows, :] / total

    packed = value[gram_rows:gram_rows + reals, :]
    moved = pltpu.roll(packed, wide - shapes, 1)
    weights = jnp.where(place < shapes, packed / jnp.sqrt(jnp.where(place < shapes, moved, 0.0) / total + EPS), 0.0)
    tall = jnp.broadcast_to(weights[:, None, :], (reals, GROUP, wide)).reshape(reals * GROUP, wide)
    hi = tall.astype(BF16)
    lo = (tall - hi.astype(F32)).astype(BF16)
    spread = spread_v[...]
    w_hi[...] = jnp.dot(hi, spread, preferred_element_type=F32).astype(BF16) * keep_v[...]
    w_lo[...] = jnp.dot(lo, spread, preferred_element_type=F32).astype(BF16) * keep_v[...]

    mine.wait()
    step = inner * own * GROUP
    for at, plane in enumerate(near_planes + far_planes):
        for e in range(inner):
            if at == 0 and e == 0:
                continue
            block_from(plane * inner + (i + e) % inner).wait_recv()
        lanes = pl.ds(pl.multiple_of(plane * step, step), step)
        left_hi, left_lo = w_hi[:, lanes], w_lo[:, lanes]
        for g in range(cols // GROUP):
            here = slice(g * GROUP, (g + 1) * GROUP)
            right = blocks[pl.ds(plane * inner, inner), :, here, :].reshape(step, rows)
            term = jnp.dot(left_hi, right, preferred_element_type=F32) + jnp.dot(
                left_lo, right, preferred_element_type=F32
            )
            term = term.reshape(reals, GROUP, rows)
            if at == 0:
                change_ref[:, here, :] = term
            else:
                change_ref[:, here, :] += term

    over.wait_send()
    for copy in crossing + sent + plane_sent + out_sent:
        copy.wait_send()


def hand_over(pieces, gram_ref, change_ref, gram_out, change_out, sems):
    part = change_ref.shape[0] // pieces
    copies = [pltpu.make_async_copy(gram_ref, gram_out, sems.at[pieces])]
    for at in range(pieces):
        here = pl.ds(at * part, part)
        copies.append(pltpu.make_async_copy(change_ref.at[here], change_out.at[here], sems.at[at]))
    for copy in copies:
        copy.start()
    for copy in copies:
        copy.wait()


def in_kernel(deviations, basis, sensitivity, blade_ids):
    count = lax.axis_size("pts")
    cores = lax.axis_size("blk")
    points, blades = deviations.shape
    shapes = basis.shape[1]
    own, rows, order = sensitivity.shape
    reals = blade_ids.shape[0]
    outer, inner = split_of(count)
    cols = order // count
    gram_rows, gram_cols = blades // count, blades // cores
    chunks = 12
    wide = 2 * shapes
    total = float(points * count * cores)
    hbm = pl.BlockSpec(memory_space=pltpu.HBM)
    vmem = pl.BlockSpec(memory_space=pltpu.VMEM)
    sem = pltpu.SemaphoreType.DMA
    body = outer * gram_rows
    flops = 2 * points * blades * (blades + shapes) + 4 * reals * shapes * GROUP * rows * cols
    gram, change = pl.pallas_call(
        functools.partial(kernel, (outer, inner, chunks, total)),
        out_shape=(pltpu.VMEM((gram_rows, gram_cols), F32), pltpu.VMEM((reals, cols, rows), F32)),
        in_specs=[hbm, hbm, hbm, hbm],
        out_specs=(vmem, vmem),
        scratch_shapes=[
            pltpu.VMEM((1, reals), jnp.int32),
            pltpu.VMEM((points, blades), BF16),
            pltpu.VMEM((shapes, points), BF16),
            pltpu.VMEM((own, rows, order), BF16),
            pltpu.VMEM((own, order, rows), BF16),
            pltpu.VMEM((count, own, cols, rows), BF16),
            pltpu.VMEM((blades, blades), F32),
            pltpu.VMEM((wide, blades), F32),
            pltpu.VMEM((wide, shapes * GROUP), BF16),
            pltpu.VMEM((reals * GROUP, shapes * GROUP), BF16),
            pltpu.VMEM((reals * GROUP, shapes * GROUP), BF16),
            pltpu.VMEM((reals * GROUP, shapes * GROUP), BF16),
            pltpu.VMEM((2, blades + reals, gram_cols), F32),
            pltpu.VMEM((blades + reals, gram_cols), F32),
            pltpu.VMEM((inner, body + reals, gram_cols), F32),
            pltpu.VMEM((inner, body + reals, gram_cols), F32),
            pltpu.VMEM((outer, gram_rows + reals, gram_cols), F32),
            pltpu.VMEM((outer, gram_rows + reals, gram_cols), F32),
            sem, sem((chunks,)), sem, sem((outer,)), sem,
            sem((count,)), sem((count,)), sem, sem,
            sem((inner,)), sem((inner,)), sem((outer,)), sem((outer,)),
        ],
        compiler_params=pltpu.CompilerParams(
            collective_id=0, has_side_effects=True, vmem_limit_bytes=32 * 1024 * 1024
        ),
        cost_estimate=pl.CostEstimate(
            flops=flops, transcendentals=0, bytes_accessed=2 * points * (blades + shapes) + 8 * own * rows * order
        ),
    )(
        pltpu.with_memory_space_constraint(blade_ids[None, :], pltpu.HBM),
        pltpu.with_memory_space_constraint(deviations, pltpu.HBM),
        pltpu.with_memory_space_constraint(basis.T, pltpu.HBM),
        pltpu.with_memory_space_constraint(sensitivity, pltpu.HBM),
    )
    pieces = 4
    gram, change = pl.pallas_call(
        functools.partial(hand_over, pieces),
        out_shape=(
            jax.ShapeDtypeStruct((gram_rows, gram_cols), F32),
            jax.ShapeDtypeStruct((reals, cols, rows), F32),
        ),
        in_specs=[vmem, vmem],
        out_specs=(hbm, hbm),
        scratch_shapes=[sem((pieces + 1,))],
        compiler_params=pltpu.CompilerParams(vmem_limit_bytes=4 * 1024 * 1024),
    )(
        pltpu.with_memory_space_constraint(gram, pltpu.VMEM),
        pltpu.with_memory_space_constraint(change, pltpu.VMEM),
    )
    return gram, jnp.transpose(change, (0, 2, 1))


def with_collectives(deviations, basis, sensitivity, blade_ids):
    total = deviations.shape[0] * lax.axis_size("pts") * lax.axis_size("blk")
    blades = deviations.shape[1]
    dims = (((0,), (0,)), ((), ()))
    term = lax.dot_general(deviations, deviations, dims, preferred_element_type=F32) / total
    row_part = lax.psum_scatter(term, "pts", scatter_dimension=0, tiled=True)
    gram = lax.psum_scatter(row_part, "blk", scatter_dimension=1, tiled=True)
    coeff_part = lax.dot_general(basis, deviations, dims, preferred_element_type=F32)
    energy_part = jnp.sum(jnp.square(deviations.astype(F32)), axis=0) / total
    selector = (jnp.arange(blades, dtype=jnp.int32)[:, None] == blade_ids[None, :]).astype(F32)
    coeffs, energy = lax.psum((coeff_part, energy_part), ("pts", "blk"))
    picked = jnp.dot(coeffs, selector, precision=lax.Precision.HIGHEST)
    picked_energy = jnp.dot(energy, selector, precision=lax.Precision.HIGHEST)
    weights = picked / jnp.sqrt(picked_energy + EPS)
    tiles = lax.all_to_all(sensitivity, "pts", split_axis=2, concat_axis=0, tiled=True)
    change = jnp.einsum("kb,kij->bij", weights, tiles.astype(F32), precision=lax.Precision.HIGHEST)
    return gram, change


def on_device(deviations, basis, sensitivity, blade_ids):
    count, cores = lax.axis_size("pts"), lax.axis_size("blk")
    points, blades = deviations.shape
    own, rows, order = sensitivity.shape
    outer, inner = split_of(count)
    fits = (
        cores == 2
        and outer * inner == count
        and outer % 2 == 0
        and (order // count) % GROUP == 0
        and (blades // count) % 8 == 0
        and (blades // cores) == 2 * basis.shape[1]
        and (blades // cores) % 128 == 0
        and rows % 128 == 0
        and (order // count * inner) % 128 == 0
        and (inner * own * GROUP) % 128 == 0
        and points % (12 * 128) == 0
        and blade_ids.shape[0] % 8 == 0
    )
    run = in_kernel if fits else with_collectives
    return run(deviations, basis, sensitivity, blade_ids)


def solution(mesh):
    in_specs = (P(("pts", "blk"), None), P(("pts", "blk"), None), P("pts", "blk", None), P())
    out_specs = (P("pts", "blk"), P(None, "blk", "pts"))
    return jax.shard_map(
        on_device, mesh=mesh, in_specs=in_specs, out_specs=out_specs, check_vma=False
    )
```

```python
import functools

import jax
import jax.numpy as jnp
from jax import lax
from jax.experimental import pallas as pl
from jax.experimental.pallas import tpu as pltpu
from jax.sharding import PartitionSpec as P

MESH = pl.DeviceIdType.MESH
F32 = jnp.float32
BF16 = jnp.bfloat16
GROUP = 16
EPS = 1e-05


def split_of(count):
    inner = 1
    while inner * inner < count:
        inner *= 2
    return count // inner, inner


def kernel(
    dims, ids_hbm, dev_hbm, basis_hbm, sens_hbm, gram_ref, change_ref,
    ids_ref, dev_v, basis_v, sens_v, turned, blocks, gram_acc, coef_acc, spread_v, keep_v, w_hi, w_lo,
    s1, r1, s2, r2, s3, r3,
    ids_sem, dev_sem, basis_sem, sens_sem, own_sem, a_send, a_recv, c_send, c_recv, x_send, x_recv, z_send, z_recv,
):
    outer, inner, chunks, total = dims
    count = outer * inner
    half = outer // 2
    me = lax.axis_index("pts")
    core = lax.axis_index("blk")
    o, i = me // inner, me % inner
    side = o // half
    reals = ids_ref.shape[1]
    points, blades = dev_hbm.shape
    shapes = basis_hbm.shape[0]
    own, rows, order = sens_hbm.shape
    cols = order // count
    part = points // chunks
    gram_rows, gram_cols = gram_ref.shape
    span = cols * inner

    barrier = pltpu.get_barrier_semaphore()
    for d in range(1, count):
        pl.semaphore_signal(barrier, inc=1, device_id=((me + d) % count, core), device_id_type=MESH)
    pl.semaphore_signal(barrier, inc=1, device_id=(me, 1 - core), device_id_type=MESH)

    far_planes = [(1 - side) * half + (o + e) % half for e in range(half)]
    near_planes = [side * half + (o + e) % half for e in range(half)]
    depth = side * (o - half) + (1 - side) * (half - 1 - o)
    middle = 1 - (2 * depth) // half
    first = [middle * n + (1 - middle) * f for n, f in zip(near_planes, far_planes)]
    second = [middle * f + (1 - middle) * n for n, f in zip(near_planes, far_planes)]
    loads = []
    for at, plane in enumerate(first + second):
        here = pl.ds(pl.multiple_of(plane * span, span), span)
        loads.append(pltpu.make_async_copy(sens_hbm.at[:, :, here], sens_v.at[:, :, here], sens_sem.at[at]))
        loads[-1].start()
    ids_load = pltpu.make_async_copy(ids_hbm, ids_ref, ids_sem)
    ids_load.start()
    basis_load = pltpu.make_async_copy(basis_hbm, basis_v, basis_sem)
    basis_load.start()

    def dev_load(c):
        at = pl.ds(pl.multiple_of(c * part, part), part)
        return pltpu.make_async_copy(dev_hbm.at[at], dev_v.at[at], dev_sem.at[c])

    for c in range(chunks):
        dev_load(c).start()

    def turn(plane):
        here = pl.ds(pl.multiple_of(plane * span, span), span)
        for k in range(own):
            turned[k, here, :] = sens_v[k, :, here].T

    def block_to(peer):
        at = pl.ds(pl.multiple_of(peer * cols, cols), cols)
        return pltpu.make_async_remote_copy(
            src_ref=turned.at[:, at, :], dst_ref=blocks.at[me], send_sem=a_send.at[peer], recv_sem=a_recv.at[me],
            device_id=(peer, core), device_id_type=MESH,
        )

    def block_from(peer):
        return pltpu.make_async_remote_copy(
            src_ref=turned.at[:, pl.ds(0, cols), :], dst_ref=blocks.at[peer], send_sem=a_send.at[peer],
            recv_sem=a_recv.at[peer], device_id=(peer, core), device_id_type=MESH,
        )

    crossing = [block_to(plane * inner + (i + e) % inner) for plane in far_planes for e in range(inner)]
    inside = [
        [block_to(plane * inner + (i + e) % inner) for e in range(inner) if at > 0 or e > 0]
        for at, plane in enumerate(near_planes)
    ]
    many = len(crossing)

    def send(outside_copies, middle_copies):
        for kind, copies in ((0, outside_copies), (1, middle_copies)):
            @pl.when(middle == kind)
            def _():
                for copy in copies:
                    copy.start()

    for at, plane in enumerate(first):
        loads[at].wait()
        turn(plane)
        if at == 0:
            pl.semaphore_wait(barrier, count)
        send(crossing[at * inner:min((at + 1) * inner, many // 2)], inside[at])
    for at, plane in enumerate(second):
        loads[half + at].wait()
        turn(plane)
    mine = pltpu.make_async_copy(
        turned.at[:, pl.ds(pl.multiple_of(me * cols, cols), cols), :], blocks.at[me], own_sem
    )
    mine.start()

    spread_v[...] = (
        lax.broadcasted_iota(jnp.int32, spread_v.shape, 1) // GROUP == lax.broadcasted_iota(jnp.int32, spread_v.shape, 0)
    ).astype(F32).astype(BF16)
    keep_v[...] = (
        lax.broadcasted_iota(jnp.int32, keep_v.shape, 0) % GROUP
        == lax.broadcasted_iota(jnp.int32, keep_v.shape, 1) % GROUP
    ).astype(F32).astype(BF16)

    gram_acc[...] = jnp.zeros_like(gram_acc)
    coef_acc[...] = jnp.zeros_like(coef_acc)
    basis_load.wait()

    def accumulate(c, carry):
        dev_load(c).wait()
        start = pl.multiple_of(c * part, part)
        block = dev_v[pl.ds(start, part), :]
        gram_acc[...] += jnp.dot(block.T, block, preferred_element_type=F32)
        coef_acc[0:shapes, :] += jnp.dot(basis_v[:, pl.ds(start, part)], block, preferred_element_type=F32)
        return carry

    lax.fori_loop(0, chunks, accumulate, 0)

    wide = coef_acc.shape[0]
    ids_load.wait()
    ids = jnp.broadcast_to(ids_ref[...].astype(F32), (reals, reals))
    square = lax.broadcasted_iota(jnp.int32, (reals, reals), 0) == lax.broadcasted_iota(jnp.int32, (reals, reals), 1)
    ids_col = jnp.sum(jnp.where(square, ids, 0.0), axis=1, keepdims=True)
    lane = lax.broadcasted_iota(jnp.int32, (reals, blades), 1).astype(F32)
    chosen = jnp.where(ids_col == lane, 1.0, 0.0).astype(F32)
    gram = gram_acc[...]
    diagonal = lax.broadcasted_iota(jnp.int32, gram.shape, 0) == lax.broadcasted_iota(jnp.int32, gram.shape, 1)
    squares = jnp.sum(jnp.where(diagonal, gram, 0.0), axis=0, keepdims=True)
    energy = jnp.sum(chosen * squares, axis=1, keepdims=True)
    picked = lax.dot_general(
        chosen, coef_acc[...], (((1,), (1,)), ((), ())), preferred_element_type=F32, precision=lax.Precision.HIGHEST
    )
    place = lax.broadcasted_iota(jnp.int32, (reals, wide), 1)
    picked = jnp.where(place < shapes, picked, energy)

    for h in range(2):
        s1[h, 0:blades, :] = gram[:, h * gram_cols:(h + 1) * gram_cols]
        s1[h, blades:blades + reals, :] = picked
    over = pltpu.make_async_remote_copy(
        src_ref=s1.at[1 - core], dst_ref=r1, send_sem=c_send, recv_sem=c_recv,
        device_id=(me, 1 - core), device_id_type=MESH,
    )
    over.start()
    send(crossing[many // 2:3 * many // 4], crossing[:many // 8])
    over.wait_recv()

    body = outer * gram_rows
    tail = s1[core, blades:blades + reals, :] + r1[blades:blades + reals, :]
    for j in range(inner):
        for q in range(outer):
            at = (q * inner + j) * gram_rows
            s2[j, q * gram_rows:(q + 1) * gram_rows, :] = (
                s1[core, at:at + gram_rows, :] + r1[at:at + gram_rows, :]
            )
        s2[j, body:body + reals, :] = tail
    plane_sent = []
    for e in range(1, inner):
        j = (i + e) % inner
        plane_sent.append(
            pltpu.make_async_remote_copy(
                src_ref=s2.at[j], dst_ref=r2.at[i], send_sem=x_send.at[j], recv_sem=x_recv.at[i],
                device_id=(o * inner + j, core), device_id_type=MESH,
            )
        )
        plane_sent[-1].start()
    send(crossing[3 * many // 4:7 * many // 8], crossing[many // 8:many // 4])
    value = s2[i]
    for e in range(1, inner):
        j = (i + e) % inner
        pltpu.make_async_remote_copy(
            src_ref=s2.at[j], dst_ref=r2.at[j], send_sem=x_send.at[j], recv_sem=x_recv.at[j],
            device_id=(o * inner + j, core), device_id_type=MESH,
        ).wait_recv()
        value = value + r2[j]

    for q in range(outer):
        s3[q, 0:gram_rows, :] = value[q * gram_rows:(q + 1) * gram_rows, :]
        s3[q, gram_rows:gram_rows + reals, :] = value[body:body + reals, :]
    out_sent = []
    for e in range(1, outer):
        q = (o + e) % outer
        out_sent.append(
            pltpu.make_async_remote_copy(
                src_ref=s3.at[q], dst_ref=r3.at[o], send_sem=z_send.at[q], recv_sem=z_recv.at[o],
                device_id=(q * inner + i, core), device_id_type=MESH,
            )
        )
        out_sent[-1].start()
    send(crossing[7 * many // 8:] + sum(inside, []), crossing[many // 4:])
    value = s3[o]
    for e in range(1, outer):
        q = (o + e) % outer
        pltpu.make_async_remote_copy(
            src_ref=s3.at[q], dst_ref=r3.at[q], send_sem=z_send.at[q], recv_sem=z_recv.at[q],
            device_id=(q * inner + i, core), device_id_type=MESH,
        ).wait_recv()
        value = value + r3[q]
    gram_ref[...] = value[0:gram_rows, :] / total

    packed = value[gram_rows:gram_rows + reals, :]
    moved = pltpu.roll(packed, wide - shapes, 1)
    weights = jnp.where(place < shapes, packed / jnp.sqrt(jnp.where(place < shapes, moved, 0.0) / total + EPS), 0.0)
    tall = jnp.broadcast_to(weights[:, None, :], (reals, GROUP, wide)).reshape(reals * GROUP, wide)
    hi = tall.astype(BF16)
    lo = (tall - hi.astype(F32)).astype(BF16)
    spread = spread_v[...]
    w_hi[...] = jnp.dot(hi, spread, preferred_element_type=F32).astype(BF16) * keep_v[...]
    w_lo[...] = jnp.dot(lo, spread, preferred_element_type=F32).astype(BF16) * keep_v[...]

    mine.wait()
    step = inner * own * GROUP
    last_planes = [side * e + (1 - side) * (outer - 1 - e) for e in range(half)]
    for at, plane in enumerate(near_planes + last_planes):
        for e in range(inner):
            if at == 0 and e == 0:
                continue
            block_from(plane * inner + (i + e) % inner).wait_recv()
        lanes = pl.ds(pl.multiple_of(plane * step, step), step)
        left_hi, left_lo = w_hi[:, lanes], w_lo[:, lanes]
        for g in range(cols // GROUP):
            here = slice(g * GROUP, (g + 1) * GROUP)
            right = blocks[pl.ds(plane * inner, inner), :, here, :].reshape(step, rows)
            term = jnp.dot(left_hi, right, preferred_element_type=F32) + jnp.dot(
                left_lo, right, preferred_element_type=F32
            )
            term = term.reshape(reals, GROUP, rows)
            if at == 0:
                change_ref[:, here, :] = term
            else:
                change_ref[:, here, :] += term

    over.wait_send()
    for copy in crossing + sum(inside, []) + plane_sent + out_sent:
        copy.wait_send()


def hand_over(pieces, gram_ref, change_ref, gram_out, change_out, sems):
    part = change_ref.shape[0] // pieces
    copies = [pltpu.make_async_copy(gram_ref, gram_out, sems.at[pieces])]
    for at in range(pieces):
        here = pl.ds(at * part, part)
        copies.append(pltpu.make_async_copy(change_ref.at[here], change_out.at[here], sems.at[at]))
    for copy in copies:
        copy.start()
    for copy in copies:
        copy.wait()


def in_kernel(deviations, basis, sensitivity, blade_ids):
    count = lax.axis_size("pts")
    cores = lax.axis_size("blk")
    points, blades = deviations.shape
    shapes = basis.shape[1]
    own, rows, order = sensitivity.shape
    reals = blade_ids.shape[0]
    outer, inner = split_of(count)
    cols = order // count
    gram_rows, gram_cols = blades // count, blades // cores
    chunks = 12
    wide = 2 * shapes
    total = float(points * count * cores)
    hbm = pl.BlockSpec(memory_space=pltpu.HBM)
    vmem = pl.BlockSpec(memory_space=pltpu.VMEM)
    sem = pltpu.SemaphoreType.DMA
    body = outer * gram_rows
    flops = 2 * points * blades * (blades + shapes) + 4 * reals * shapes * GROUP * rows * cols
    gram, change = pl.pallas_call(
        functools.partial(kernel, (outer, inner, chunks, total)),
        out_shape=(pltpu.VMEM((gram_rows, gram_cols), F32), pltpu.VMEM((reals, cols, rows), F32)),
        in_specs=[hbm, hbm, hbm, hbm],
        out_specs=(vmem, vmem),
        scratch_shapes=[
            pltpu.VMEM((1, reals), jnp.int32),
            pltpu.VMEM((points, blades), BF16),
            pltpu.VMEM((shapes, points), BF16),
            pltpu.VMEM((own, rows, order), BF16),
            pltpu.VMEM((own, order, rows), BF16),
            pltpu.VMEM((count, own, cols, rows), BF16),
            pltpu.VMEM((blades, blades), F32),
            pltpu.VMEM((wide, blades), F32),
            pltpu.VMEM((wide, shapes * GROUP), BF16),
            pltpu.VMEM((reals * GROUP, shapes * GROUP), BF16),
            pltpu.VMEM((reals * GROUP, shapes * GROUP), BF16),
            pltpu.VMEM((reals * GROUP, shapes * GROUP), BF16),
            pltpu.VMEM((2, blades + reals, gram_cols), F32),
            pltpu.VMEM((blades + reals, gram_cols), F32),
            pltpu.VMEM((inner, body + reals, gram_cols), F32),
            pltpu.VMEM((inner, body + reals, gram_cols), F32),
            pltpu.VMEM((outer, gram_rows + reals, gram_cols), F32),
            pltpu.VMEM((outer, gram_rows + reals, gram_cols), F32),
            sem, sem((chunks,)), sem, sem((outer,)), sem,
            sem((count,)), sem((count,)), sem, sem,
            sem((inner,)), sem((inner,)), sem((outer,)), sem((outer,)),
        ],
        compiler_params=pltpu.CompilerParams(
            collective_id=0, has_side_effects=True, vmem_limit_bytes=32 * 1024 * 1024
        ),
        cost_estimate=pl.CostEstimate(
            flops=flops, transcendentals=0, bytes_accessed=2 * points * (blades + shapes) + 8 * own * rows * order
        ),
    )(
        pltpu.with_memory_space_constraint(blade_ids[None, :], pltpu.HBM),
        pltpu.with_memory_space_constraint(deviations, pltpu.HBM),
        pltpu.with_memory_space_constraint(basis.T, pltpu.HBM),
        pltpu.with_memory_space_constraint(sensitivity, pltpu.HBM),
    )
    pieces = 4
    gram, change = pl.pallas_call(
        functools.partial(hand_over, pieces),
        out_shape=(
            jax.ShapeDtypeStruct((gram_rows, gram_cols), F32),
            jax.ShapeDtypeStruct((reals, cols, rows), F32),
        ),
        in_specs=[vmem, vmem],
        out_specs=(hbm, hbm),
        scratch_shapes=[sem((pieces + 1,))],
        compiler_params=pltpu.CompilerParams(vmem_limit_bytes=4 * 1024 * 1024),
    )(
        pltpu.with_memory_space_constraint(gram, pltpu.VMEM),
        pltpu.with_memory_space_constraint(change, pltpu.VMEM),
    )
    return gram, jnp.transpose(change, (0, 2, 1))


def with_collectives(deviations, basis, sensitivity, blade_ids):
    total = deviations.shape[0] * lax.axis_size("pts") * lax.axis_size("blk")
    blades = deviations.shape[1]
    dims = (((0,), (0,)), ((), ()))
    term = lax.dot_general(deviations, deviations, dims, preferred_element_type=F32) / total
    row_part = lax.psum_scatter(term, "pts", scatter_dimension=0, tiled=True)
    gram = lax.psum_scatter(row_part, "blk", scatter_dimension=1, tiled=True)
    coeff_part = lax.dot_general(basis, deviations, dims, preferred_element_type=F32)
    energy_part = jnp.sum(jnp.square(deviations.astype(F32)), axis=0) / total
    selector = (jnp.arange(blades, dtype=jnp.int32)[:, None] == blade_ids[None, :]).astype(F32)
    coeffs, energy = lax.psum((coeff_part, energy_part), ("pts", "blk"))
    picked = jnp.dot(coeffs, selector, precision=lax.Precision.HIGHEST)
    picked_energy = jnp.dot(energy, selector, precision=lax.Precision.HIGHEST)
    weights = picked / jnp.sqrt(picked_energy + EPS)
    tiles = lax.all_to_all(sensitivity, "pts", split_axis=2, concat_axis=0, tiled=True)
    change = jnp.einsum("kb,kij->bij", weights, tiles.astype(F32), precision=lax.Precision.HIGHEST)
    return gram, change


def on_device(deviations, basis, sensitivity, blade_ids):
    count, cores = lax.axis_size("pts"), lax.axis_size("blk")
    points, blades = deviations.shape
    own, rows, order = sensitivity.shape
    outer, inner = split_of(count)
    fits = (
        cores == 2
        and outer * inner == count
        and outer % 2 == 0
        and (order // count) % GROUP == 0
        and (blades // count) % 8 == 0
        and (blades // cores) == 2 * basis.shape[1]
        and (blades // cores) % 128 == 0
        and rows % 128 == 0
        and (order // count * inner) % 128 == 0
        and (inner * own * GROUP) % 128 == 0
        and points % (12 * 128) == 0
        and blade_ids.shape[0] % 8 == 0
    )
    run = in_kernel if fits else with_collectives
    return run(deviations, basis, sensitivity, blade_ids)


def solution(mesh):
    in_specs = (P(("pts", "blk"), None), P(("pts", "blk"), None), P("pts", "blk", None), P())
    out_specs = (P("pts", "blk"), P(None, "blk", "pts"))
    return jax.shard_map(
        on_device, mesh=mesh, in_specs=in_specs, out_specs=out_specs, check_vma=False
    )
```

```python
import functools

import jax
import jax.numpy as jnp
from jax import lax
from jax.experimental import pallas as pl
from jax.experimental.pallas import tpu as pltpu
from jax.sharding import PartitionSpec as P

MESH = pl.DeviceIdType.MESH
F32 = jnp.float32
BF16 = jnp.bfloat16
GROUP = 16
EPS = 1e-05


def split_of(count):
    inner = 1
    while inner * inner < count:
        inner *= 2
    return count // inner, inner


def kernel(
    dims, ids_hbm, dev_hbm, basis_hbm, sens_hbm, gram_ref, change_ref,
    ids_ref, dev_v, basis_v, sens_v, turned, blocks, coef_acc, spread_v, keep_v, w_hi, w_lo,
    s1, r1, s2, r2, s3, r3,
    ids_sem, dev_sem, basis_sem, sens_sem, own_sem, a_send, a_recv, c_send, c_recv, x_send, x_recv, z_send, z_recv,
):
    outer, inner, chunks, total = dims
    count = outer * inner
    half = outer // 2
    me = lax.axis_index("pts")
    core = lax.axis_index("blk")
    o, i = me // inner, me % inner
    side = o // half
    reals = ids_ref.shape[1]
    points, blades = dev_hbm.shape
    shapes = basis_hbm.shape[0]
    own, rows, order = sens_hbm.shape
    cols = order // count
    part = points // chunks
    gram_rows, gram_cols = gram_ref.shape
    span = cols * inner

    barrier = pltpu.get_barrier_semaphore()
    for d in range(1, count):
        pl.semaphore_signal(barrier, inc=1, device_id=((me + d) % count, core), device_id_type=MESH)
    pl.semaphore_signal(barrier, inc=1, device_id=(me, 1 - core), device_id_type=MESH)

    far_planes = [(1 - side) * half + (o + e) % half for e in range(half)]
    near_planes = [side * half + (o + e) % half for e in range(half)]
    planes = [plane for pair in zip(near_planes, far_planes) for plane in pair]
    loads = []
    for at, plane in enumerate(planes):
        here = pl.ds(pl.multiple_of(plane * span, span), span)
        loads.append(pltpu.make_async_copy(sens_hbm.at[:, :, here], sens_v.at[:, :, here], sens_sem.at[at]))
        loads[-1].start()
    ids_load = pltpu.make_async_copy(ids_hbm, ids_ref, ids_sem)
    ids_load.start()
    basis_load = pltpu.make_async_copy(basis_hbm, basis_v, basis_sem)
    basis_load.start()

    def dev_load(c):
        at = pl.ds(c * part, part)
        return pltpu.make_async_copy(dev_hbm.at[at], dev_v.at[at], dev_sem.at[c])

    for c in range(chunks):
        dev_load(c).start()

    def turn(plane):
        here = pl.ds(pl.multiple_of(plane * span, span), span)
        for k in range(own):
            turned[k, here, :] = sens_v[k, :, here].T

    def block_to(peer):
        at = pl.ds(pl.multiple_of(peer * cols, cols), cols)
        return pltpu.make_async_remote_copy(
            src_ref=turned.at[:, at, :], dst_ref=blocks.at[me], send_sem=a_send.at[peer], recv_sem=a_recv.at[me],
            device_id=(peer, core), device_id_type=MESH,
        )

    def block_from(peer):
        return pltpu.make_async_remote_copy(
            src_ref=turned.at[:, pl.ds(0, cols), :], dst_ref=blocks.at[peer], send_sem=a_send.at[peer],
            recv_sem=a_recv.at[peer], device_id=(peer, core), device_id_type=MESH,
        )

    inside = [plane * inner + (i + e) % inner for plane in near_planes for e in range(inner)][1:]
    crossing = [plane * inner + (i + e) % inner for plane in far_planes for e in range(inner)]
    sent = [block_to(peer) for pair in zip(crossing, inside + [None]) for peer in pair if peer is not None]
    swapped = [sent[at ^ 1] for at in range(len(sent) - 1)] + sent[-1:]
    done = 0

    def send(amount):
        nonlocal done
        here = slice(done, done + amount)
        done += amount
        for kind, copies in ((0, sent[here]), (1, swapped[here])):
            @pl.when(core == kind)
            def _():
                for copy in copies:
                    copy.start()

    for at, plane in enumerate(planes):
        loads[at].wait()
        turn(plane)
        if at == 1:
            pl.semaphore_wait(barrier, count)
            send(4)
    mine = pltpu.make_async_copy(
        turned.at[:, pl.ds(pl.multiple_of(me * cols, cols), cols), :], blocks.at[me], own_sem
    )
    mine.start()
    send(2)

    spread_v[...] = (
        lax.broadcasted_iota(jnp.int32, spread_v.shape, 1) // GROUP == lax.broadcasted_iota(jnp.int32, spread_v.shape, 0)
    ).astype(F32).astype(BF16)
    keep_v[...] = (
        lax.broadcasted_iota(jnp.int32, keep_v.shape, 0) % GROUP
        == lax.broadcasted_iota(jnp.int32, keep_v.shape, 1) % GROUP
    ).astype(F32).astype(BF16)

    basis_load.wait()
    gram, coef = 0.0, 0.0
    for c in range(chunks):
        dev_load(c).wait()
        at = slice(c * part, (c + 1) * part)
        block = dev_v[at, :]
        gram = gram + jnp.dot(block.T, block, preferred_element_type=F32)
        coef = coef + jnp.dot(basis_v[:, at], block, preferred_element_type=F32)
    coef_acc[0:shapes, :] = coef
    coef_acc[shapes:, :] = jnp.zeros_like(coef_acc[shapes:, :])

    wide = coef_acc.shape[0]
    ids_load.wait()
    ids = jnp.broadcast_to(ids_ref[...].astype(F32), (reals, reals))
    square = lax.broadcasted_iota(jnp.int32, (reals, reals), 0) == lax.broadcasted_iota(jnp.int32, (reals, reals), 1)
    ids_col = jnp.sum(jnp.where(square, ids, 0.0), axis=1, keepdims=True)
    lane = lax.broadcasted_iota(jnp.int32, (reals, blades), 1).astype(F32)
    chosen = jnp.where(ids_col == lane, 1.0, 0.0).astype(F32)
    diagonal = lax.broadcasted_iota(jnp.int32, gram.shape, 0) == lax.broadcasted_iota(jnp.int32, gram.shape, 1)
    squares = jnp.sum(jnp.where(diagonal, gram, 0.0), axis=0, keepdims=True)
    energy = jnp.sum(chosen * squares, axis=1, keepdims=True)
    picked = lax.dot_general(
        chosen, coef_acc[...], (((1,), (1,)), ((), ())), preferred_element_type=F32, precision=lax.Precision.HIGHEST
    )
    place = lax.broadcasted_iota(jnp.int32, (reals, wide), 1)
    picked = jnp.where(place < shapes, picked, energy)

    for h in range(2):
        s1[h, 0:blades, :] = gram[:, h * gram_cols:(h + 1) * gram_cols]
        s1[h, blades:blades + reals, :] = picked
    over = pltpu.make_async_remote_copy(
        src_ref=s1.at[1 - core], dst_ref=r1, send_sem=c_send, recv_sem=c_recv,
        device_id=(me, 1 - core), device_id_type=MESH,
    )
    over.start()
    send(2)
    over.wait_recv()

    body = outer * gram_rows
    tail = s1[core, blades:blades + reals, :] + r1[blades:blades + reals, :]
    for j in range(inner):
        for q in range(outer):
            at = (q * inner + j) * gram_rows
            s2[j, q * gram_rows:(q + 1) * gram_rows, :] = (
                s1[core, at:at + gram_rows, :] + r1[at:at + gram_rows, :]
            )
        s2[j, body:body + reals, :] = tail
    plane_sent = []
    for e in range(1, inner):
        j = (i + e) % inner
        plane_sent.append(
            pltpu.make_async_remote_copy(
                src_ref=s2.at[j], dst_ref=r2.at[i], send_sem=x_send.at[j], recv_sem=x_recv.at[i],
                device_id=(o * inner + j, core), device_id_type=MESH,
            )
        )
        plane_sent[-1].start()
    send(2)
    value = s2[i]
    for e in range(1, inner):
        j = (i + e) % inner
        pltpu.make_async_remote_copy(
            src_ref=s2.at[j], dst_ref=r2.at[j], send_sem=x_send.at[j], recv_sem=x_recv.at[j],
            device_id=(o * inner + j, core), device_id_type=MESH,
        ).wait_recv()
        value = value + r2[j]

    for q in range(outer):
        s3[q, 0:gram_rows, :] = value[q * gram_rows:(q + 1) * gram_rows, :]
        s3[q, gram_rows:gram_rows + reals, :] = value[body:body + reals, :]
    out_sent = []
    for e in range(1, outer):
        q = (o + e) % outer
        out_sent.append(
            pltpu.make_async_remote_copy(
                src_ref=s3.at[q], dst_ref=r3.at[o], send_sem=z_send.at[q], recv_sem=z_recv.at[o],
                device_id=(q * inner + i, core), device_id_type=MESH,
            )
        )
        out_sent[-1].start()
    send(len(sent) - done)
    value = s3[o]
    for e in range(1, outer):
        q = (o + e) % outer
        pltpu.make_async_remote_copy(
            src_ref=s3.at[q], dst_ref=r3.at[q], send_sem=z_send.at[q], recv_sem=z_recv.at[q],
            device_id=(q * inner + i, core), device_id_type=MESH,
        ).wait_recv()
        value = value + r3[q]
    gram_ref[...] = value[0:gram_rows, :] / total

    packed = value[gram_rows:gram_rows + reals, :]
    moved = pltpu.roll(packed, wide - shapes, 1)
    weights = jnp.where(place < shapes, packed / jnp.sqrt(jnp.where(place < shapes, moved, 0.0) / total + EPS), 0.0)
    tall = jnp.broadcast_to(weights[:, None, :], (reals, GROUP, wide)).reshape(reals * GROUP, wide)
    hi = tall.astype(BF16)
    lo = (tall - hi.astype(F32)).astype(BF16)
    spread = spread_v[...]
    w_hi[...] = jnp.dot(hi, spread, preferred_element_type=F32).astype(BF16) * keep_v[...]
    w_lo[...] = jnp.dot(lo, spread, preferred_element_type=F32).astype(BF16) * keep_v[...]

    mine.wait()
    step = inner * own * GROUP
    for at, plane in enumerate(planes):
        for e in range(inner):
            if at == 0 and e == 0:
                continue
            block_from(plane * inner + (i + e) % inner).wait_recv()
        lanes = pl.ds(pl.multiple_of(plane * step, step), step)
        left_hi, left_lo = w_hi[:, lanes], w_lo[:, lanes]
        for g in range(cols // GROUP):
            here = slice(g * GROUP, (g + 1) * GROUP)
            right = blocks[pl.ds(plane * inner, inner), :, here, :].reshape(step, rows)
            term = jnp.dot(left_hi, right, preferred_element_type=F32) + jnp.dot(
                left_lo, right, preferred_element_type=F32
            )
            term = term.reshape(reals, GROUP, rows)
            if at == 0:
                change_ref[:, here, :] = term
            else:
                change_ref[:, here, :] += term

    over.wait_send()
    for copy in sent + plane_sent + out_sent:
        copy.wait_send()


def hand_over(pieces, gram_ref, change_ref, gram_out, change_out, sems):
    part = change_ref.shape[0] // pieces
    copies = [pltpu.make_async_copy(gram_ref, gram_out, sems.at[pieces])]
    for at in range(pieces):
        here = pl.ds(at * part, part)
        copies.append(pltpu.make_async_copy(change_ref.at[here], change_out.at[here], sems.at[at]))
    for copy in copies:
        copy.start()
    for copy in copies:
        copy.wait()


def in_kernel(deviations, basis, sensitivity, blade_ids):
    count = lax.axis_size("pts")
    cores = lax.axis_size("blk")
    points, blades = deviations.shape
    shapes = basis.shape[1]
    own, rows, order = sensitivity.shape
    reals = blade_ids.shape[0]
    outer, inner = split_of(count)
    cols = order // count
    gram_rows, gram_cols = blades // count, blades // cores
    chunks = 4
    wide = 2 * shapes
    total = float(points * count * cores)
    hbm = pl.BlockSpec(memory_space=pltpu.HBM)
    vmem = pl.BlockSpec(memory_space=pltpu.VMEM)
    sem = pltpu.SemaphoreType.DMA
    body = outer * gram_rows
    flops = 2 * points * blades * (blades + shapes) + 4 * reals * shapes * GROUP * rows * cols
    gram, change = pl.pallas_call(
        functools.partial(kernel, (outer, inner, chunks, total)),
        out_shape=(pltpu.VMEM((gram_rows, gram_cols), F32), pltpu.VMEM((reals, cols, rows), F32)),
        in_specs=[hbm, hbm, hbm, hbm],
        out_specs=(vmem, vmem),
        scratch_shapes=[
            pltpu.VMEM((1, reals), jnp.int32),
            pltpu.VMEM((points, blades), BF16),
            pltpu.VMEM((shapes, points), BF16),
            pltpu.VMEM((own, rows, order), BF16),
            pltpu.VMEM((own, order, rows), BF16),
            pltpu.VMEM((count, own, cols, rows), BF16),
            pltpu.VMEM((wide, blades), F32),
            pltpu.VMEM((wide, shapes * GROUP), BF16),
            pltpu.VMEM((reals * GROUP, shapes * GROUP), BF16),
            pltpu.VMEM((reals * GROUP, shapes * GROUP), BF16),
            pltpu.VMEM((reals * GROUP, shapes * GROUP), BF16),
            pltpu.VMEM((2, blades + reals, gram_cols), F32),
            pltpu.VMEM((blades + reals, gram_cols), F32),
            pltpu.VMEM((inner, body + reals, gram_cols), F32),
            pltpu.VMEM((inner, body + reals, gram_cols), F32),
            pltpu.VMEM((outer, gram_rows + reals, gram_cols), F32),
            pltpu.VMEM((outer, gram_rows + reals, gram_cols), F32),
            sem, sem((chunks,)), sem, sem((outer,)), sem,
            sem((count,)), sem((count,)), sem, sem,
            sem((inner,)), sem((inner,)), sem((outer,)), sem((outer,)),
        ],
        compiler_params=pltpu.CompilerParams(
            collective_id=0, has_side_effects=True, vmem_limit_bytes=32 * 1024 * 1024
        ),
        cost_estimate=pl.CostEstimate(
            flops=flops, transcendentals=0, bytes_accessed=2 * points * (blades + shapes) + 8 * own * rows * order
        ),
    )(
        pltpu.with_memory_space_constraint(blade_ids[None, :], pltpu.HBM),
        pltpu.with_memory_space_constraint(deviations, pltpu.HBM),
        pltpu.with_memory_space_constraint(basis.T, pltpu.HBM),
        pltpu.with_memory_space_constraint(sensitivity, pltpu.HBM),
    )
    pieces = 4
    gram, change = pl.pallas_call(
        functools.partial(hand_over, pieces),
        out_shape=(
            jax.ShapeDtypeStruct((gram_rows, gram_cols), F32),
            jax.ShapeDtypeStruct((reals, cols, rows), F32),
        ),
        in_specs=[vmem, vmem],
        out_specs=(hbm, hbm),
        scratch_shapes=[sem((pieces + 1,))],
        compiler_params=pltpu.CompilerParams(vmem_limit_bytes=4 * 1024 * 1024),
    )(
        pltpu.with_memory_space_constraint(gram, pltpu.VMEM),
        pltpu.with_memory_space_constraint(change, pltpu.VMEM),
    )
    return gram, jnp.transpose(change, (0, 2, 1))


def with_collectives(deviations, basis, sensitivity, blade_ids):
    total = deviations.shape[0] * lax.axis_size("pts") * lax.axis_size("blk")
    blades = deviations.shape[1]
    dims = (((0,), (0,)), ((), ()))
    term = lax.dot_general(deviations, deviations, dims, preferred_element_type=F32) / total
    row_part = lax.psum_scatter(term, "pts", scatter_dimension=0, tiled=True)
    gram = lax.psum_scatter(row_part, "blk", scatter_dimension=1, tiled=True)
    coeff_part = lax.dot_general(basis, deviations, dims, preferred_element_type=F32)
    energy_part = jnp.sum(jnp.square(deviations.astype(F32)), axis=0) / total
    selector = (jnp.arange(blades, dtype=jnp.int32)[:, None] == blade_ids[None, :]).astype(F32)
    coeffs, energy = lax.psum((coeff_part, energy_part), ("pts", "blk"))
    picked = jnp.dot(coeffs, selector, precision=lax.Precision.HIGHEST)
    picked_energy = jnp.dot(energy, selector, precision=lax.Precision.HIGHEST)
    weights = picked / jnp.sqrt(picked_energy + EPS)
    tiles = lax.all_to_all(sensitivity, "pts", split_axis=2, concat_axis=0, tiled=True)
    change = jnp.einsum("kb,kij->bij", weights, tiles.astype(F32), precision=lax.Precision.HIGHEST)
    return gram, change


def on_device(deviations, basis, sensitivity, blade_ids):
    count, cores = lax.axis_size("pts"), lax.axis_size("blk")
    points, blades = deviations.shape
    own, rows, order = sensitivity.shape
    outer, inner = split_of(count)
    fits = (
        cores == 2
        and outer * inner == count
        and outer % 2 == 0
        and (order // count) % GROUP == 0
        and (blades // count) % 8 == 0
        and (blades // cores) == 2 * basis.shape[1]
        and (blades // cores) % 128 == 0
        and rows % 128 == 0
        and (order // count * inner) % 128 == 0
        and (inner * own * GROUP) % 128 == 0
        and points % (4 * 128) == 0
        and blade_ids.shape[0] % 8 == 0
    )
    run = in_kernel if fits else with_collectives
    return run(deviations, basis, sensitivity, blade_ids)


def solution(mesh):
    in_specs = (P(("pts", "blk"), None), P(("pts", "blk"), None), P("pts", "blk", None), P())
    out_specs = (P("pts", "blk"), P(None, "blk", "pts"))
    return jax.shard_map(
        on_device, mesh=mesh, in_specs=in_specs, out_specs=out_specs, check_vma=False
    )
```

```python
import functools

import jax
import jax.numpy as jnp
from jax import lax
from jax.experimental import pallas as pl
from jax.experimental.pallas import tpu as pltpu
from jax.sharding import PartitionSpec as P

MESH = pl.DeviceIdType.MESH
F32 = jnp.float32
BF16 = jnp.bfloat16
GROUP = 16
EPS = 1e-05


def split_of(count):
    inner = 1
    while inner * inner < count:
        inner *= 2
    return count // inner, inner


def kernel(
    dims, ids_hbm, dev_hbm, basis_hbm, sens_hbm, gram_ref, change_ref,
    ids_ref, dev_v, basis_v, sens_v, turned, blocks, coef_acc, spread_v, keep_v, w_hi, w_lo,
    s1, r1, s2, r2, s3, r3,
    ids_sem, dev_sem, basis_sem, sens_sem, own_sem, a_send, a_recv, c_send, c_recv, x_send, x_recv, z_send, z_recv,
):
    outer, inner, chunks, total = dims
    count = outer * inner
    half = outer // 2
    me = lax.axis_index("pts")
    core = lax.axis_index("blk")
    o, i = me // inner, me % inner
    side = o // half
    reals = ids_ref.shape[1]
    points, blades = dev_hbm.shape
    shapes = basis_hbm.shape[0]
    own, rows, order = sens_hbm.shape
    cols = order // count
    part = points // chunks
    gram_rows, gram_cols = gram_ref.shape
    span = cols * inner

    far_planes = [(1 - side) * half + (o + e) % half for e in range(half)]
    near_planes = [side * half + (o + e) % half for e in range(half)]
    planes = [plane for pair in zip(near_planes, far_planes) for plane in pair]
    turns = [
        plane for n, f in zip(near_planes, far_planes) for plane in (core * n + (1 - core) * f, core * f + (1 - core) * n)
    ]
    loads = []
    for at, plane in enumerate(turns):
        here = pl.ds(pl.multiple_of(plane * span, span), span)
        loads.append(pltpu.make_async_copy(sens_hbm.at[:, :, here], sens_v.at[:, :, here], sens_sem.at[at]))
    loads[0].start()

    barrier = pltpu.get_barrier_semaphore()
    for d in range(1, count):
        pl.semaphore_signal(barrier, inc=1, device_id=((me + d) % count, core), device_id_type=MESH)
    pl.semaphore_signal(barrier, inc=1, device_id=(me, 1 - core), device_id_type=MESH)
    for load in loads[1:]:
        load.start()
    ids_load = pltpu.make_async_copy(ids_hbm, ids_ref, ids_sem)
    ids_load.start()
    basis_load = pltpu.make_async_copy(basis_hbm, basis_v, basis_sem)
    basis_load.start()

    def dev_load(c):
        at = pl.ds(c * part, part)
        return pltpu.make_async_copy(dev_hbm.at[at], dev_v.at[at], dev_sem.at[c])

    for c in range(chunks):
        dev_load(c).start()

    def turn(plane):
        here = pl.ds(pl.multiple_of(plane * span, span), span)
        for k in range(own):
            turned[k, here, :] = sens_v[k, :, here].T

    def block_to(peer):
        at = pl.ds(pl.multiple_of(peer * cols, cols), cols)
        return pltpu.make_async_remote_copy(
            src_ref=turned.at[:, at, :], dst_ref=blocks.at[me], send_sem=a_send.at[peer], recv_sem=a_recv.at[me],
            device_id=(peer, core), device_id_type=MESH,
        )

    def block_from(peer):
        return pltpu.make_async_remote_copy(
            src_ref=turned.at[:, pl.ds(0, cols), :], dst_ref=blocks.at[peer], send_sem=a_send.at[peer],
            recv_sem=a_recv.at[peer], device_id=(peer, core), device_id_type=MESH,
        )

    pairs = inner // 2
    peers = [(i // 2 + h) % pairs * 2 + (i + b) % 2 for h in range(pairs) for b in range(2)]

    inside = [plane * inner + peer for plane in near_planes for peer in peers][1:]
    crossing = [plane * inner + peer for plane in far_planes for peer in peers]
    sent = [block_to(peer) for pair in zip(crossing, inside + [None]) for peer in pair if peer is not None]
    swapped = [sent[at ^ 1] for at in range(len(sent) - 1)] + sent[-1:]
    sent[1], sent[2] = sent[2], sent[1]
    swapped[1], swapped[2] = swapped[2], swapped[1]
    done = 0

    def send(amount):
        nonlocal done
        here = slice(done, done + amount)
        done += amount
        for kind, copies in ((0, sent[here]), (1, swapped[here])):
            @pl.when(core == kind)
            def _():
                for copy in copies:
                    copy.start()

    for at, plane in enumerate(turns):
        loads[at].wait()
        turn(plane)
        if at == 0:
            pl.semaphore_wait(barrier, count)
        if at < 2:
            send(2)
    mine = pltpu.make_async_copy(
        turned.at[:, pl.ds(pl.multiple_of(me * cols, cols), cols), :], blocks.at[me], own_sem
    )
    mine.start()
    send(2)

    spread_v[...] = (
        lax.broadcasted_iota(jnp.int32, spread_v.shape, 1) // GROUP == lax.broadcasted_iota(jnp.int32, spread_v.shape, 0)
    ).astype(F32).astype(BF16)
    keep_v[...] = (
        lax.broadcasted_iota(jnp.int32, keep_v.shape, 0) % GROUP
        == lax.broadcasted_iota(jnp.int32, keep_v.shape, 1) % GROUP
    ).astype(F32).astype(BF16)

    basis_load.wait()
    gram, coef = 0.0, 0.0
    for c in range(chunks):
        dev_load(c).wait()
        at = slice(c * part, (c + 1) * part)
        block = dev_v[at, :]
        gram = gram + jnp.dot(block.T, block, preferred_element_type=F32)
        coef = coef + jnp.dot(basis_v[:, at], block, preferred_element_type=F32)
    coef_acc[0:shapes, :] = coef
    coef_acc[shapes:, :] = jnp.zeros_like(coef_acc[shapes:, :])

    wide = coef_acc.shape[0]
    ids_load.wait()
    ids = jnp.broadcast_to(ids_ref[...].astype(F32), (reals, reals))
    square = lax.broadcasted_iota(jnp.int32, (reals, reals), 0) == lax.broadcasted_iota(jnp.int32, (reals, reals), 1)
    ids_col = jnp.sum(jnp.where(square, ids, 0.0), axis=1, keepdims=True)
    lane = lax.broadcasted_iota(jnp.int32, (reals, blades), 1).astype(F32)
    chosen = jnp.where(ids_col == lane, 1.0, 0.0).astype(F32)
    diagonal = lax.broadcasted_iota(jnp.int32, gram.shape, 0) == lax.broadcasted_iota(jnp.int32, gram.shape, 1)
    squares = jnp.sum(jnp.where(diagonal, gram, 0.0), axis=0, keepdims=True)
    energy = jnp.sum(chosen * squares, axis=1, keepdims=True)
    picked = lax.dot_general(
        chosen, coef_acc[...], (((1,), (1,)), ((), ())), preferred_element_type=F32, precision=lax.Precision.HIGHEST
    )
    place = lax.broadcasted_iota(jnp.int32, (reals, wide), 1)
    picked = jnp.where(place < shapes, picked, energy)

    for h in range(2):
        s1[h, 0:blades, :] = gram[:, h * gram_cols:(h + 1) * gram_cols]
        s1[h, blades:blades + reals, :] = picked
    over = pltpu.make_async_remote_copy(
        src_ref=s1.at[1 - core], dst_ref=r1, send_sem=c_send, recv_sem=c_recv,
        device_id=(me, 1 - core), device_id_type=MESH,
    )
    over.start()
    send(2)
    over.wait_recv()

    body = outer * gram_rows
    tail = s1[core, blades:blades + reals, :] + r1[blades:blades + reals, :]
    for j in range(inner):
        for q in range(outer):
            at = (q * inner + j) * gram_rows
            s2[j, q * gram_rows:(q + 1) * gram_rows, :] = (
                s1[core, at:at + gram_rows, :] + r1[at:at + gram_rows, :]
            )
        s2[j, body:body + reals, :] = tail
    plane_sent = []
    for e in range(1, inner):
        j = (i + e) % inner
        plane_sent.append(
            pltpu.make_async_remote_copy(
                src_ref=s2.at[j], dst_ref=r2.at[i], send_sem=x_send.at[j], recv_sem=x_recv.at[i],
                device_id=(o * inner + j, core), device_id_type=MESH,
            )
        )
        plane_sent[-1].start()
    send(2)
    value = s2[i]
    for e in range(1, inner):
        j = (i + e) % inner
        pltpu.make_async_remote_copy(
            src_ref=s2.at[j], dst_ref=r2.at[j], send_sem=x_send.at[j], recv_sem=x_recv.at[j],
            device_id=(o * inner + j, core), device_id_type=MESH,
        ).wait_recv()
        value = value + r2[j]

    for q in range(outer):
        s3[q, 0:gram_rows, :] = value[q * gram_rows:(q + 1) * gram_rows, :]
        s3[q, gram_rows:gram_rows + reals, :] = value[body:body + reals, :]
    out_sent = []
    for e in range(1, outer):
        q = (o + e) % outer
        out_sent.append(
            pltpu.make_async_remote_copy(
                src_ref=s3.at[q], dst_ref=r3.at[o], send_sem=z_send.at[q], recv_sem=z_recv.at[o],
                device_id=(q * inner + i, core), device_id_type=MESH,
            )
        )
        out_sent[-1].start()
    send(len(sent) - done)
    value = s3[o]
    for e in range(1, outer):
        q = (o + e) % outer
        pltpu.make_async_remote_copy(
            src_ref=s3.at[q], dst_ref=r3.at[q], send_sem=z_send.at[q], recv_sem=z_recv.at[q],
            device_id=(q * inner + i, core), device_id_type=MESH,
        ).wait_recv()
        value = value + r3[q]
    gram_ref[...] = value[0:gram_rows, :] / total

    packed = value[gram_rows:gram_rows + reals, :]
    moved = pltpu.roll(packed, wide - shapes, 1)
    weights = jnp.where(place < shapes, packed / jnp.sqrt(jnp.where(place < shapes, moved, 0.0) / total + EPS), 0.0)
    tall = jnp.broadcast_to(weights[:, None, :], (reals, GROUP, wide)).reshape(reals * GROUP, wide)
    hi = tall.astype(BF16)
    lo = (tall - hi.astype(F32)).astype(BF16)
    spread = spread_v[...]
    w_hi[...] = jnp.dot(hi, spread, preferred_element_type=F32).astype(BF16) * keep_v[...]
    w_lo[...] = jnp.dot(lo, spread, preferred_element_type=F32).astype(BF16) * keep_v[...]

    mine.wait()
    step = 2 * own * GROUP
    for at, plane in enumerate(planes):
        for h in range(pairs):
            pair = plane * pairs + (i // 2 + pairs - h) % pairs
            for b in range(2):
                if at == 0 and h == 0 and b == 0:
                    continue
                block_from(pair * 2 + (i + b) % 2).wait_recv()
            lanes = pl.ds(pl.multiple_of(pair * step, step), step)
            left = jnp.concatenate([w_hi[:, lanes], w_lo[:, lanes]], axis=1)
            for g in range(cols // GROUP):
                here = slice(g * GROUP, (g + 1) * GROUP)
                right = blocks[pl.ds(pair * 2, 2), :, here, :].reshape(step, rows)
                right = jnp.concatenate([right, right], axis=0)
                term = jnp.dot(left, right, preferred_element_type=F32).reshape(reals, GROUP, rows)
                if at == 0 and h == 0:
                    change_ref[:, here, :] = term
                else:
                    change_ref[:, here, :] += term

    over.wait_send()
    for copy in sent + plane_sent + out_sent:
        copy.wait_send()


def hand_over(pieces, gram_ref, change_ref, gram_out, change_out, sems):
    part = change_ref.shape[0] // pieces
    copies = [pltpu.make_async_copy(gram_ref, gram_out, sems.at[pieces])]
    for at in range(pieces):
        here = pl.ds(at * part, part)
        copies.append(pltpu.make_async_copy(change_ref.at[here], change_out.at[here], sems.at[at]))
    for copy in copies:
        copy.start()
    for copy in copies:
        copy.wait()


def in_kernel(deviations, basis, sensitivity, blade_ids):
    count = lax.axis_size("pts")
    cores = lax.axis_size("blk")
    points, blades = deviations.shape
    shapes = basis.shape[1]
    own, rows, order = sensitivity.shape
    reals = blade_ids.shape[0]
    outer, inner = split_of(count)
    cols = order // count
    gram_rows, gram_cols = blades // count, blades // cores
    chunks = 4
    wide = 2 * shapes
    total = float(points * count * cores)
    hbm = pl.BlockSpec(memory_space=pltpu.HBM)
    vmem = pl.BlockSpec(memory_space=pltpu.VMEM)
    sem = pltpu.SemaphoreType.DMA
    body = outer * gram_rows
    flops = 2 * points * blades * (blades + shapes) + 4 * reals * shapes * GROUP * rows * cols
    gram, change = pl.pallas_call(
        functools.partial(kernel, (outer, inner, chunks, total)),
        out_shape=(pltpu.VMEM((gram_rows, gram_cols), F32), pltpu.VMEM((reals, cols, rows), F32)),
        in_specs=[hbm, hbm, hbm, hbm],
        out_specs=(vmem, vmem),
        scratch_shapes=[
            pltpu.VMEM((1, reals), jnp.int32),
            pltpu.VMEM((points, blades), BF16),
            pltpu.VMEM((shapes, points), BF16),
            pltpu.VMEM((own, rows, order), BF16),
            pltpu.VMEM((own, order, rows), BF16),
            pltpu.VMEM((count, own, cols, rows), BF16),
            pltpu.VMEM((wide, blades), F32),
            pltpu.VMEM((wide, shapes * GROUP), BF16),
            pltpu.VMEM((reals * GROUP, shapes * GROUP), BF16),
            pltpu.VMEM((reals * GROUP, shapes * GROUP), BF16),
            pltpu.VMEM((reals * GROUP, shapes * GROUP), BF16),
            pltpu.VMEM((2, blades + reals, gram_cols), F32),
            pltpu.VMEM((blades + reals, gram_cols), F32),
            pltpu.VMEM((inner, body + reals, gram_cols), F32),
            pltpu.VMEM((inner, body + reals, gram_cols), F32),
            pltpu.VMEM((outer, gram_rows + reals, gram_cols), F32),
            pltpu.VMEM((outer, gram_rows + reals, gram_cols), F32),
            sem, sem((chunks,)), sem, sem((outer,)), sem,
            sem((count,)), sem((count,)), sem, sem,
            sem((inner,)), sem((inner,)), sem((outer,)), sem((outer,)),
        ],
        compiler_params=pltpu.CompilerParams(
            collective_id=0, has_side_effects=True, vmem_limit_bytes=32 * 1024 * 1024
        ),
        cost_estimate=pl.CostEstimate(
            flops=flops, transcendentals=0, bytes_accessed=2 * points * (blades + shapes) + 8 * own * rows * order
        ),
    )(
        pltpu.with_memory_space_constraint(blade_ids[None, :], pltpu.HBM),
        pltpu.with_memory_space_constraint(deviations, pltpu.HBM),
        pltpu.with_memory_space_constraint(basis.T, pltpu.HBM),
        pltpu.with_memory_space_constraint(sensitivity, pltpu.HBM),
    )
    pieces = 4
    gram, change = pl.pallas_call(
        functools.partial(hand_over, pieces),
        out_shape=(
            jax.ShapeDtypeStruct((gram_rows, gram_cols), F32),
            jax.ShapeDtypeStruct((reals, cols, rows), F32),
        ),
        in_specs=[vmem, vmem],
        out_specs=(hbm, hbm),
        scratch_shapes=[sem((pieces + 1,))],
        compiler_params=pltpu.CompilerParams(vmem_limit_bytes=4 * 1024 * 1024),
    )(
        pltpu.with_memory_space_constraint(gram, pltpu.VMEM),
        pltpu.with_memory_space_constraint(change, pltpu.VMEM),
    )
    return gram, jnp.transpose(change, (0, 2, 1))


def with_collectives(deviations, basis, sensitivity, blade_ids):
    total = deviations.shape[0] * lax.axis_size("pts") * lax.axis_size("blk")
    blades = deviations.shape[1]
    dims = (((0,), (0,)), ((), ()))
    term = lax.dot_general(deviations, deviations, dims, preferred_element_type=F32) / total
    row_part = lax.psum_scatter(term, "pts", scatter_dimension=0, tiled=True)
    gram = lax.psum_scatter(row_part, "blk", scatter_dimension=1, tiled=True)
    coeff_part = lax.dot_general(basis, deviations, dims, preferred_element_type=F32)
    energy_part = jnp.sum(jnp.square(deviations.astype(F32)), axis=0) / total
    selector = (jnp.arange(blades, dtype=jnp.int32)[:, None] == blade_ids[None, :]).astype(F32)
    coeffs, energy = lax.psum((coeff_part, energy_part), ("pts", "blk"))
    picked = jnp.dot(coeffs, selector, precision=lax.Precision.HIGHEST)
    picked_energy = jnp.dot(energy, selector, precision=lax.Precision.HIGHEST)
    weights = picked / jnp.sqrt(picked_energy + EPS)
    tiles = lax.all_to_all(sensitivity, "pts", split_axis=2, concat_axis=0, tiled=True)
    change = jnp.einsum("kb,kij->bij", weights, tiles.astype(F32), precision=lax.Precision.HIGHEST)
    return gram, change


def on_device(deviations, basis, sensitivity, blade_ids):
    count, cores = lax.axis_size("pts"), lax.axis_size("blk")
    points, blades = deviations.shape
    own, rows, order = sensitivity.shape
    outer, inner = split_of(count)
    fits = (
        cores == 2
        and outer * inner == count
        and outer % 2 == 0
        and (order // count) % GROUP == 0
        and (blades // count) % 8 == 0
        and (blades // cores) == 2 * basis.shape[1]
        and (blades // cores) % 128 == 0
        and rows % 128 == 0
        and (order // count * inner) % 128 == 0
        and inner % 2 == 0
        and (2 * own * GROUP) % 128 == 0
        and points % (4 * 128) == 0
        and blade_ids.shape[0] % 8 == 0
    )
    run = in_kernel if fits else with_collectives
    return run(deviations, basis, sensitivity, blade_ids)


def solution(mesh):
    in_specs = (P(("pts", "blk"), None), P(("pts", "blk"), None), P("pts", "blk", None), P())
    out_specs = (P("pts", "blk"), P(None, "blk", "pts"))
    return jax.shard_map(
        on_device, mesh=mesh, in_specs=in_specs, out_specs=out_specs, check_vma=False
    )
```

```python
import functools

import jax
import jax.numpy as jnp
from jax import lax
from jax.experimental import pallas as pl
from jax.experimental.pallas import tpu as pltpu
from jax.sharding import PartitionSpec as P

MESH = pl.DeviceIdType.MESH
F32 = jnp.float32
BF16 = jnp.bfloat16
GROUP = 16
EPS = 1e-05


def split_of(count):
    inner = 1
    while inner * inner < count:
        inner *= 2
    return count // inner, inner


def kernel(
    dims, ids_hbm, dev_hbm, basis_hbm, sens_hbm, gram_ref, change_ref,
    ids_ref, dev_v, basis_v, sens_v, turned, blocks, coef_acc, spread_v, keep_v, w_hi, w_lo,
    s1, r1, s2, r2, s3, r3, s4, r4,
    ids_sem, dev_sem, basis_sem, sens_sem, own_sem, a_send, a_recv, c_send, c_recv, x_send, x_recv, z_send, z_recv,
    m_send, m_recv,
):
    outer, inner, chunks, total = dims
    count = outer * inner
    half = outer // 2
    me = lax.axis_index("pts")
    core = lax.axis_index("blk")
    o, i = me // inner, me % inner
    side = o // half
    reals = ids_ref.shape[1]
    points, blades = dev_hbm.shape
    shapes = basis_hbm.shape[0]
    own, rows, order = sens_hbm.shape
    cols = order // count
    part = points // chunks
    gram_rows, gram_cols = gram_ref.shape
    span = cols * inner

    far_planes = [(1 - side) * half + (o + e) % half for e in range(half)]
    near_planes = [side * half + (o + e) % half for e in range(half)]
    planes = [plane for pair in zip(near_planes, far_planes) for plane in pair]
    turns = [
        plane for n, f in zip(near_planes, far_planes) for plane in (core * n + (1 - core) * f, core * f + (1 - core) * n)
    ]
    loads = []
    for at, plane in enumerate(turns):
        here = pl.ds(pl.multiple_of(plane * span, span), span)
        loads.append(pltpu.make_async_copy(sens_hbm.at[:, :, here], sens_v.at[:, :, here], sens_sem.at[at]))
    loads[0].start()

    barrier = pltpu.get_barrier_semaphore()
    for d in range(1, count):
        pl.semaphore_signal(barrier, inc=1, device_id=((me + d) % count, core), device_id_type=MESH)
    pl.semaphore_signal(barrier, inc=1, device_id=(me, 1 - core), device_id_type=MESH)
    for load in loads[1:]:
        load.start()
    ids_load = pltpu.make_async_copy(ids_hbm, ids_ref, ids_sem)
    ids_load.start()
    basis_load = pltpu.make_async_copy(basis_hbm, basis_v, basis_sem)
    basis_load.start()

    def dev_load(c):
        at = pl.ds(c * part, part)
        return pltpu.make_async_copy(dev_hbm.at[at], dev_v.at[at], dev_sem.at[c])

    for c in range(chunks):
        dev_load(c).start()

    def turn(plane):
        here = pl.ds(pl.multiple_of(plane * span, span), span)
        for k in range(own):
            turned[k, here, :] = sens_v[k, :, here].T

    def block_to(peer):
        at = pl.ds(pl.multiple_of(peer * cols, cols), cols)
        return pltpu.make_async_remote_copy(
            src_ref=turned.at[:, at, :], dst_ref=blocks.at[me], send_sem=a_send.at[peer], recv_sem=a_recv.at[me],
            device_id=(peer, core), device_id_type=MESH,
        )

    def block_from(peer):
        return pltpu.make_async_remote_copy(
            src_ref=turned.at[:, pl.ds(0, cols), :], dst_ref=blocks.at[peer], send_sem=a_send.at[peer],
            recv_sem=a_recv.at[peer], device_id=(peer, core), device_id_type=MESH,
        )

    pairs = inner // 2
    peers = [(i // 2 + h) % pairs * 2 + (i + b) % 2 for h in range(pairs) for b in range(2)]

    inside = [plane * inner + peer for plane in near_planes for peer in peers][1:]
    crossing = [plane * inner + peer for plane in far_planes for peer in peers]
    sent = [block_to(peer) for pair in zip(crossing, inside + [None]) for peer in pair if peer is not None]
    swapped = [sent[at ^ 1] for at in range(len(sent) - 1)] + sent[-1:]
    sent[1], sent[2] = sent[2], sent[1]
    swapped[1], swapped[2] = swapped[2], swapped[1]
    done = 0

    def send(amount):
        nonlocal done
        here = slice(done, done + amount)
        done += amount
        for kind, copies in ((0, sent[here]), (1, swapped[here])):
            @pl.when(core == kind)
            def _():
                for copy in copies:
                    copy.start()

    for at, plane in enumerate(turns):
        loads[at].wait()
        turn(plane)
        if at == 0:
            pl.semaphore_wait(barrier, count)
        if at < 2:
            send(2)
    mine = pltpu.make_async_copy(
        turned.at[:, pl.ds(pl.multiple_of(me * cols, cols), cols), :], blocks.at[me], own_sem
    )
    mine.start()
    send(2)

    spread_v[...] = (
        lax.broadcasted_iota(jnp.int32, spread_v.shape, 1) // GROUP == lax.broadcasted_iota(jnp.int32, spread_v.shape, 0)
    ).astype(F32).astype(BF16)
    keep_v[...] = (
        lax.broadcasted_iota(jnp.int32, keep_v.shape, 0) % GROUP
        == lax.broadcasted_iota(jnp.int32, keep_v.shape, 1) % GROUP
    ).astype(F32).astype(BF16)

    basis_load.wait()
    gram, coef = 0.0, 0.0
    for c in range(chunks):
        dev_load(c).wait()
        at = slice(c * part, (c + 1) * part)
        block = dev_v[at, :]
        gram = gram + jnp.dot(block.T, block, preferred_element_type=F32)
        coef = coef + jnp.dot(basis_v[:, at], block, preferred_element_type=F32)
    coef_acc[0:shapes, :] = coef
    coef_acc[shapes:, :] = jnp.zeros_like(coef_acc[shapes:, :])

    wide = coef_acc.shape[0]
    ids_load.wait()
    ids = jnp.broadcast_to(ids_ref[...].astype(F32), (reals, reals))
    square = lax.broadcasted_iota(jnp.int32, (reals, reals), 0) == lax.broadcasted_iota(jnp.int32, (reals, reals), 1)
    ids_col = jnp.sum(jnp.where(square, ids, 0.0), axis=1, keepdims=True)
    lane = lax.broadcasted_iota(jnp.int32, (reals, blades), 1).astype(F32)
    chosen = jnp.where(ids_col == lane, 1.0, 0.0).astype(F32)
    diagonal = lax.broadcasted_iota(jnp.int32, gram.shape, 0) == lax.broadcasted_iota(jnp.int32, gram.shape, 1)
    squares = jnp.sum(jnp.where(diagonal, gram, 0.0), axis=0, keepdims=True)
    energy = jnp.sum(chosen * squares, axis=1, keepdims=True)
    picked = lax.dot_general(
        chosen, coef_acc[...], (((1,), (1,)), ((), ())), preferred_element_type=F32, precision=lax.Precision.HIGHEST
    )
    place = lax.broadcasted_iota(jnp.int32, (reals, wide), 1)
    picked = jnp.where(place < shapes, picked, energy)

    for h in range(2):
        s1[h, 0:blades, :] = gram[:, h * gram_cols:(h + 1) * gram_cols]
        s1[h, blades:blades + reals, :] = picked
    over = pltpu.make_async_remote_copy(
        src_ref=s1.at[1 - core], dst_ref=r1, send_sem=c_send, recv_sem=c_recv,
        device_id=(me, 1 - core), device_id_type=MESH,
    )
    over.start()
    send(2)
    over.wait_recv()

    body = outer * gram_rows
    tail = s1[core, blades:blades + reals, :] + r1[blades:blades + reals, :]
    for j in range(inner):
        for q in range(outer):
            at = (q * inner + j) * gram_rows
            s2[j, q * gram_rows:(q + 1) * gram_rows, :] = (
                s1[core, at:at + gram_rows, :] + r1[at:at + gram_rows, :]
            )
        s2[j, body:body + reals, :] = tail
    plane_sent = []
    for e in range(1, inner):
        j = (i + e) % inner
        plane_sent.append(
            pltpu.make_async_remote_copy(
                src_ref=s2.at[j], dst_ref=r2.at[i], send_sem=x_send.at[j], recv_sem=x_recv.at[i],
                device_id=(o * inner + j, core), device_id_type=MESH,
            )
        )
        plane_sent[-1].start()
    send(2)
    value = s2[i]
    for e in range(1, inner):
        j = (i + e) % inner
        pltpu.make_async_remote_copy(
            src_ref=s2.at[j], dst_ref=r2.at[j], send_sem=x_send.at[j], recv_sem=x_recv.at[j],
            device_id=(o * inner + j, core), device_id_type=MESH,
        ).wait_recv()
        value = value + r2[j]

    r2[i] = value
    place_in_half = o % half
    for n in range(half):
        for at, plane in enumerate((side * half + n, (1 - side) * half + n)):
            there = pl.ds(pl.multiple_of(plane * gram_rows, gram_rows), gram_rows)
            s3[n, at * gram_rows:(at + 1) * gram_rows, :] = r2[i, there, :]
        s3[n, 2 * gram_rows:2 * gram_rows + reals, :] = value[body:body + reals, :]
    out_sent = []
    for e in range(1, half):
        n = (place_in_half + e) % half
        out_sent.append(
            pltpu.make_async_remote_copy(
                src_ref=s3.at[n], dst_ref=r3.at[place_in_half], send_sem=z_send.at[n],
                recv_sem=z_recv.at[place_in_half],
                device_id=((side * half + n) * inner + i, core), device_id_type=MESH,
            )
        )
        out_sent[-1].start()
    send(1)
    value = s3[place_in_half]
    for e in range(1, half):
        n = (place_in_half + e) % half
        pltpu.make_async_remote_copy(
            src_ref=s3.at[n], dst_ref=r3.at[n], send_sem=z_send.at[n], recv_sem=z_recv.at[n],
            device_id=((side * half + n) * inner + i, core), device_id_type=MESH,
        ).wait_recv()
        value = value + r3[n]

    s4[0:gram_rows, :] = value[gram_rows:2 * gram_rows, :]
    s4[gram_rows:gram_rows + reals, :] = value[2 * gram_rows:2 * gram_rows + reals, :]
    out_sent.append(
        pltpu.make_async_remote_copy(
            src_ref=s4, dst_ref=r4, send_sem=m_send, recv_sem=m_recv,
            device_id=((o + half) % outer * inner + i, core), device_id_type=MESH,
        )
    )
    out_sent[-1].start()
    send(len(sent) - done)
    out_sent[-1].wait_recv()
    gram_ref[...] = (value[0:gram_rows, :] + r4[0:gram_rows, :]) / total
    packed = value[2 * gram_rows:2 * gram_rows + reals, :] + r4[gram_rows:gram_rows + reals, :]

    moved = pltpu.roll(packed, wide - shapes, 1)
    weights = jnp.where(place < shapes, packed / jnp.sqrt(jnp.where(place < shapes, moved, 0.0) / total + EPS), 0.0)
    tall = jnp.broadcast_to(weights[:, None, :], (reals, GROUP, wide)).reshape(reals * GROUP, wide)
    hi = tall.astype(BF16)
    lo = (tall - hi.astype(F32)).astype(BF16)
    spread = spread_v[...]
    w_hi[...] = jnp.dot(hi, spread, preferred_element_type=F32).astype(BF16) * keep_v[...]
    w_lo[...] = jnp.dot(lo, spread, preferred_element_type=F32).astype(BF16) * keep_v[...]

    mine.wait()
    step = 2 * own * GROUP
    for at, plane in enumerate(planes):
        for h in range(pairs):
            pair = plane * pairs + (i // 2 + pairs - h) % pairs
            for b in range(2):
                if at == 0 and h == 0 and b == 0:
                    continue
                block_from(pair * 2 + (i + b) % 2).wait_recv()
            lanes = pl.ds(pl.multiple_of(pair * step, step), step)
            left = jnp.concatenate([w_hi[:, lanes], w_lo[:, lanes]], axis=1)
            for g in range(cols // GROUP):
                here = slice(g * GROUP, (g + 1) * GROUP)
                right = blocks[pl.ds(pair * 2, 2), :, here, :].reshape(step, rows)
                right = jnp.concatenate([right, right], axis=0)
                term = jnp.dot(left, right, preferred_element_type=F32).reshape(reals, GROUP, rows)
                if at == 0 and h == 0:
                    change_ref[:, here, :] = term
                else:
                    change_ref[:, here, :] += term

    over.wait_send()
    for copy in sent + plane_sent + out_sent:
        copy.wait_send()


def hand_over(pieces, gram_ref, change_ref, gram_out, change_out, sems):
    part = change_ref.shape[0] // pieces
    copies = [pltpu.make_async_copy(gram_ref, gram_out, sems.at[pieces])]
    for at in range(pieces):
        here = pl.ds(at * part, part)
        copies.append(pltpu.make_async_copy(change_ref.at[here], change_out.at[here], sems.at[at]))
    for copy in copies:
        copy.start()
    for copy in copies:
        copy.wait()


def in_kernel(deviations, basis, sensitivity, blade_ids):
    count = lax.axis_size("pts")
    cores = lax.axis_size("blk")
    points, blades = deviations.shape
    shapes = basis.shape[1]
    own, rows, order = sensitivity.shape
    reals = blade_ids.shape[0]
    outer, inner = split_of(count)
    cols = order // count
    gram_rows, gram_cols = blades // count, blades // cores
    chunks = 4
    wide = 2 * shapes
    total = float(points * count * cores)
    hbm = pl.BlockSpec(memory_space=pltpu.HBM)
    vmem = pl.BlockSpec(memory_space=pltpu.VMEM)
    sem = pltpu.SemaphoreType.DMA
    body = outer * gram_rows
    flops = 2 * points * blades * (blades + shapes) + 4 * reals * shapes * GROUP * rows * cols
    gram, change = pl.pallas_call(
        functools.partial(kernel, (outer, inner, chunks, total)),
        out_shape=(pltpu.VMEM((gram_rows, gram_cols), F32), pltpu.VMEM((reals, cols, rows), F32)),
        in_specs=[hbm, hbm, hbm, hbm],
        out_specs=(vmem, vmem),
        scratch_shapes=[
            pltpu.VMEM((1, reals), jnp.int32),
            pltpu.VMEM((points, blades), BF16),
            pltpu.VMEM((shapes, points), BF16),
            pltpu.VMEM((own, rows, order), BF16),
            pltpu.VMEM((own, order, rows), BF16),
            pltpu.VMEM((count, own, cols, rows), BF16),
            pltpu.VMEM((wide, blades), F32),
            pltpu.VMEM((wide, shapes * GROUP), BF16),
            pltpu.VMEM((reals * GROUP, shapes * GROUP), BF16),
            pltpu.VMEM((reals * GROUP, shapes * GROUP), BF16),
            pltpu.VMEM((reals * GROUP, shapes * GROUP), BF16),
            pltpu.VMEM((2, blades + reals, gram_cols), F32),
            pltpu.VMEM((blades + reals, gram_cols), F32),
            pltpu.VMEM((inner, body + reals, gram_cols), F32),
            pltpu.VMEM((inner, body + reals, gram_cols), F32),
            pltpu.VMEM((outer // 2, 2 * gram_rows + reals, gram_cols), F32),
            pltpu.VMEM((outer // 2, 2 * gram_rows + reals, gram_cols), F32),
            pltpu.VMEM((gram_rows + reals, gram_cols), F32),
            pltpu.VMEM((gram_rows + reals, gram_cols), F32),
            sem, sem((chunks,)), sem, sem((outer,)), sem,
            sem((count,)), sem((count,)), sem, sem,
            sem((inner,)), sem((inner,)), sem((outer // 2,)), sem((outer // 2,)), sem, sem,
        ],
        compiler_params=pltpu.CompilerParams(
            collective_id=0, has_side_effects=True, vmem_limit_bytes=32 * 1024 * 1024
        ),
        cost_estimate=pl.CostEstimate(
            flops=flops, transcendentals=0, bytes_accessed=2 * points * (blades + shapes) + 8 * own * rows * order
        ),
    )(
        pltpu.with_memory_space_constraint(blade_ids[None, :], pltpu.HBM),
        pltpu.with_memory_space_constraint(deviations, pltpu.HBM),
        pltpu.with_memory_space_constraint(basis.T, pltpu.HBM),
        pltpu.with_memory_space_constraint(sensitivity, pltpu.HBM),
    )
    pieces = 4
    gram, change = pl.pallas_call(
        functools.partial(hand_over, pieces),
        out_shape=(
            jax.ShapeDtypeStruct((gram_rows, gram_cols), F32),
            jax.ShapeDtypeStruct((reals, cols, rows), F32),
        ),
        in_specs=[vmem, vmem],
        out_specs=(hbm, hbm),
        scratch_shapes=[sem((pieces + 1,))],
        compiler_params=pltpu.CompilerParams(vmem_limit_bytes=4 * 1024 * 1024),
    )(
        pltpu.with_memory_space_constraint(gram, pltpu.VMEM),
        pltpu.with_memory_space_constraint(change, pltpu.VMEM),
    )
    return gram, jnp.transpose(change, (0, 2, 1))


def with_collectives(deviations, basis, sensitivity, blade_ids):
    total = deviations.shape[0] * lax.axis_size("pts") * lax.axis_size("blk")
    blades = deviations.shape[1]
    dims = (((0,), (0,)), ((), ()))
    term = lax.dot_general(deviations, deviations, dims, preferred_element_type=F32) / total
    row_part = lax.psum_scatter(term, "pts", scatter_dimension=0, tiled=True)
    gram = lax.psum_scatter(row_part, "blk", scatter_dimension=1, tiled=True)
    coeff_part = lax.dot_general(basis, deviations, dims, preferred_element_type=F32)
    energy_part = jnp.sum(jnp.square(deviations.astype(F32)), axis=0) / total
    selector = (jnp.arange(blades, dtype=jnp.int32)[:, None] == blade_ids[None, :]).astype(F32)
    coeffs, energy = lax.psum((coeff_part, energy_part), ("pts", "blk"))
    picked = jnp.dot(coeffs, selector, precision=lax.Precision.HIGHEST)
    picked_energy = jnp.dot(energy, selector, precision=lax.Precision.HIGHEST)
    weights = picked / jnp.sqrt(picked_energy + EPS)
    tiles = lax.all_to_all(sensitivity, "pts", split_axis=2, concat_axis=0, tiled=True)
    change = jnp.einsum("kb,kij->bij", weights, tiles.astype(F32), precision=lax.Precision.HIGHEST)
    return gram, change


def on_device(deviations, basis, sensitivity, blade_ids):
    count, cores = lax.axis_size("pts"), lax.axis_size("blk")
    points, blades = deviations.shape
    own, rows, order = sensitivity.shape
    outer, inner = split_of(count)
    fits = (
        cores == 2
        and outer * inner == count
        and outer % 2 == 0
        and (order // count) % GROUP == 0
        and (blades // count) % 8 == 0
        and (blades // cores) == 2 * basis.shape[1]
        and (blades // cores) % 128 == 0
        and rows % 128 == 0
        and (order // count * inner) % 128 == 0
        and inner % 2 == 0
        and (2 * own * GROUP) % 128 == 0
        and points % (4 * 128) == 0
        and blade_ids.shape[0] % 8 == 0
    )
    run = in_kernel if fits else with_collectives
    return run(deviations, basis, sensitivity, blade_ids)


def solution(mesh):
    in_specs = (P(("pts", "blk"), None), P(("pts", "blk"), None), P("pts", "blk", None), P())
    out_specs = (P("pts", "blk"), P(None, "blk", "pts"))
    return jax.shard_map(
        on_device, mesh=mesh, in_specs=in_specs, out_specs=out_specs, check_vma=False
    )
```
